512 devices in a mesh: group: 8 (over y), dev: 64 (over x, z, core).
Axes of the slice: x: 4, y: 8, z: 8, core: 2. Of those that a mesh axis runs over, the one named last changes fastest.
Arguments:
- coords: float32 [3, 32, 256, 128], P(None, 'group', 'dev'), as said below
- charges: float32 [8, 32, 256, 128], P(None, 'group', 'dev'), may hold values from -6 to 6
- leaf_order: int32 [32, 256, 128], P('group', 'dev'), may hold values from 0 to 2047, as said below
- near_list: int32 [27, 32, 256, 4], P(None, 'group', 'dev'), may hold values from -1 to 32767, as said below
- far_list: int32 [138, 32, 256, 4], P(None, 'group', 'dev'), may hold values from -1 to 32767, as said below
- coarse_list: int32 [32, 16, 128, 2], P(None, 'group', 'dev'), may hold values from -1 to 4095, as said below
Outputs:
- potential: float32 [8, 32, 256, 128], P(None, 'group', 'dev')
The draws below stay inside these ranges and needn't reach their ends.
Inputs may be any that keep to these rules, and one draw needn't show every extreme that they name: `leaf_order`: within each block of 4 x 4 rows every position of the block appears once. `coords`: A point of leaf box (i, j, k) lies within 0.75 of (i + 0.5, j + 0.5, k + 0.5) in every coordinate. `near_list`: -1 marks an empty slot; other entries are distinct box numbers (i * 256 + j) * 4 + k at most one box away in each dimension, the box itself among them. `far_list`: -1 marks an empty slot; other entries are distinct box numbers at most three boxes away in each dimension, none of them in the box's near_list. `coarse_list`: -1 marks an empty slot; other entries are distinct parent numbers (i * 128 + j) * 2 + k at most two parents away in each dimension.
All inputs are finite; a program needn't handle non-finite values.
Results may differ from the reference program's by a relative error of at most 0.0033.
Values may be sent and summed in bfloat16 or wider, within the bound.
A program may use at most 192 MiB of HBM per device.

```python
import math
import jax
import jax.numpy as jnp
from jax import lax

BX = 4
BY = 4
LZ = 4
LEAF_PTS = 32
ORDER = 4
RHS = 8
NEAR = 27
FAR0 = 138
FAR1 = 32
LX = 32
LY = 256
PX = 16
PY = 128
PZ = 2


def leaf_jitter(key):
    return jax.random.randint(jax.random.fold_in(key, 101), (3, LX, LY, LZ), -2, 3).astype(jnp.int32)


def block_order(key):
    count_x = LX // BX
    count_y = LY // BY
    block_size = BX * BY * LZ * LEAF_PTS
    sub_keys = jax.random.split(jax.random.fold_in(key, 102), count_x * count_y)
    permuted = jax.vmap(lambda sub_key: jax.random.permutation(sub_key, block_size))(sub_keys).astype(jnp.int32)
    return permuted.reshape(count_x, count_y, BX, BY, LZ * LEAF_PTS).transpose(0, 2, 1, 3, 4).reshape(LX, LY, LZ * LEAF_PTS)


def shuffle_slots(entries, slots, key):
    first_key, second_key = jax.random.split(key)
    span_total = entries.shape[0]
    scores = jax.random.randint(first_key, entries.shape, 0, 2 ** 18) * 512 + jnp.arange(span_total, dtype=jnp.int32).reshape((span_total, 1, 1, 1))
    scores = jnp.where(entries >= 0, scores, scores + 2 ** 28)
    picked = jnp.take_along_axis(entries, jnp.argsort(scores, axis=0)[:slots], axis=0)
    reshuffle = jax.random.randint(second_key, picked.shape, 0, 2 ** 18) * 512 + jnp.arange(slots, dtype=jnp.int32).reshape((slots, 1, 1, 1))
    return jnp.take_along_axis(picked, jnp.argsort(reshuffle, axis=0), axis=0).astype(jnp.int32)


def neighbour_entries(jitter):
    pos_x = jnp.arange(LX, dtype=jnp.int32)[:, None, None]
    pos_y = jnp.arange(LY, dtype=jnp.int32)[None, :, None]
    pos_z = jnp.arange(LZ, dtype=jnp.int32)[None, None, :]
    padded_jitter = jnp.pad(jitter, ((0, 0), (3, 3), (3, 3), (3, 3)))
    near_rows = []
    far_rows = []
    for shift_x in range(-3, 4):
        for shift_y in range(-3, 4):
            for shift_z in range(-3, 4):
                other = padded_jitter[:, 3 + shift_x:3 + shift_x + LX, 3 + shift_y:3 + shift_y + LY, 3 + shift_z:3 + shift_z + LZ]
                target_x = pos_x + shift_x
                target_y = pos_y + shift_y
                target_z = pos_z + shift_z
                inside = (target_x >= 0) & (target_x < LX) & (target_y >= 0) & (target_y < LY) & (target_z >= 0) & (target_z < LZ)
                gap_x = 8 * shift_x + other[0] - jitter[0]
                gap_y = 8 * shift_y + other[1] - jitter[1]
                gap_z = 8 * shift_z + other[2] - jitter[2]
                close = gap_x * gap_x + gap_y * gap_y + gap_z * gap_z <= 150
                touching = max(abs(shift_x), abs(shift_y), abs(shift_z)) <= 1
                is_near = inside & close & touching
                adjacent = (jnp.abs(target_x // 2 - pos_x // 2) <= 1) & (jnp.abs(target_y // 2 - pos_y // 2) <= 1) & (jnp.abs(target_z // 2 - pos_z // 2) <= 1)
                is_far = inside & adjacent & jnp.logical_not(is_near)
                ident = (target_x * LY + target_y) * LZ + target_z
                if touching:
                    near_rows.append(jnp.where(is_near, ident, -1))
                far_rows.append(jnp.where(is_far, ident, -1))
    return (jnp.stack(near_rows).astype(jnp.int32), jnp.stack(far_rows).astype(jnp.int32))


def draw_coords(key, part):
    jitter = leaf_jitter(key)
    leaf_perm = block_order(key)
    key = jax.random.fold_in(key, 5)
    spread = jax.random.uniform(key, (3, LX, LY, LZ, LEAF_PTS), jnp.float32, -1.0, 1.0)
    centre_x = jnp.broadcast_to((jnp.arange(LX, dtype=jnp.float32) + 0.5)[:, None, None], (LX, LY, LZ))
    centre_y = jnp.broadcast_to((jnp.arange(LY, dtype=jnp.float32) + 0.5)[None, :, None], (LX, LY, LZ))
    centre_z = jnp.broadcast_to((jnp.arange(LZ, dtype=jnp.float32) + 0.5)[None, None, :], (LX, LY, LZ))
    centres = jnp.stack([centre_x, centre_y, centre_z]) + jitter.astype(jnp.float32) / 8.0
    placed = (centres[..., None] + 0.5 * spread).reshape(3, LX, LY, LZ * LEAF_PTS)
    count_x = LX // BX
    count_y = LY // BY
    row_width = LZ * LEAF_PTS
    block_size = BX * BY * row_width
    blocks = placed.reshape(3, count_x, BX, count_y, BY, row_width).transpose(1, 3, 0, 2, 4, 5).reshape(count_x, count_y, 3, block_size)
    perm_blocks = leaf_perm.reshape(count_x, BX, count_y, BY, row_width).transpose(0, 2, 1, 3, 4).reshape(count_x, count_y, 1, block_size)
    inverse = jnp.argsort(perm_blocks, axis=3)
    unsorted = jnp.take_along_axis(blocks, jnp.broadcast_to(inverse, blocks.shape), axis=3)
    return unsorted.reshape(count_x, count_y, 3, BX, BY, row_width).transpose(2, 0, 3, 1, 4, 5).reshape(3, LX, LY, row_width).astype(jnp.float32)


def draw_leaf_order(key, part):
    return block_order(key)


def draw_near_list(key, part):
    jitter = leaf_jitter(key)
    key = jax.random.fold_in(key, 7)
    near_rows, far_rows = neighbour_entries(jitter)
    return shuffle_slots(near_rows, NEAR, key)


def draw_far_list(key, part):
    jitter = leaf_jitter(key)
    key = jax.random.fold_in(key, 8)
    near_rows, far_rows = neighbour_entries(jitter)
    return shuffle_slots(far_rows, FAR0, key)


def draw_coarse_list(key, part):
    key = jax.random.fold_in(key, 9)
    jitter = jax.random.randint(jax.random.fold_in(key, 1), (3, PX, PY, PZ), -2, 3).astype(jnp.int32)
    pos_x = jnp.arange(PX, dtype=jnp.int32)[:, None, None]
    pos_y = jnp.arange(PY, dtype=jnp.int32)[None, :, None]
    pos_z = jnp.arange(PZ, dtype=jnp.int32)[None, None, :]
    padded_jitter = jnp.pad(jitter, ((0, 0), (2, 2), (2, 2), (2, 2)))
    rows = []
    for shift_x in range(-2, 3):
        for shift_y in range(-2, 3):
            for shift_z in range(-2, 3):
                if max(abs(shift_x), abs(shift_y), abs(shift_z)) == 2:
                    other = padded_jitter[:, 2 + shift_x:2 + shift_x + PX, 2 + shift_y:2 + shift_y + PY, 2 + shift_z:2 + shift_z + PZ]
                    target_x = pos_x + shift_x
                    target_y = pos_y + shift_y
                    target_z = pos_z + shift_z
                    inside = (target_x >= 0) & (target_x < PX) & (target_y >= 0) & (target_y < PY) & (target_z >= 0) & (target_z < PZ)
                    gap_x = 8 * shift_x + other[0] - jitter[0]
                    gap_y = 8 * shift_y + other[1] - jitter[1]
                    gap_z = 8 * shift_z + other[2] - jitter[2]
                    close = gap_x * gap_x + gap_y * gap_y + gap_z * gap_z <= 600
                    ident = (target_x * PY + target_y) * PZ + target_z
                    rows.append(jnp.where(inside & close, ident, -1))
    return shuffle_slots(jnp.stack(rows).astype(jnp.int32), FAR1, jax.random.fold_in(key, 2))


def levels(stream_key, shape, cuts, least, top_value):
    loudness, own = 1.0, jax.random.fold_in(stream_key, 6)
    for axis_at, blocks in cuts:
        steps = jnp.exp(jax.random.uniform(jax.random.fold_in(own, axis_at), (blocks,), jnp.float32, least / len(cuts), top_value / len(cuts)))
        loudness = loudness * jnp.repeat(steps, shape[axis_at] // blocks).reshape([-1 if axis == axis_at else 1 for axis in range(len(shape))])
    return loudness


def noise(stream_key, extent, scale, bound, shards=(), kind=jnp.bfloat16):
    drawn = scale * jax.random.normal(stream_key, extent, jnp.float32)
    if shards:
        drawn = drawn * levels(stream_key, extent, shards, -0.22, 0.18)
    return jnp.clip(drawn, -bound, bound).astype(kind)


def setup_inputs(seed: int = 0) -> dict:
    keys = jax.random.split(jax.random.key(seed), 7)
    return {
        "coords": draw_coords(jax.random.fold_in(keys[6], 71), 0),
        "charges": noise(keys[1], (RHS, LX, LY, LZ * LEAF_PTS), 1.0, 6.0, ((1, 8), (2, 64)), jnp.float32),
        "leaf_order": draw_leaf_order(jax.random.fold_in(keys[6], 71), 0),
        "near_list": draw_near_list(jax.random.fold_in(keys[6], 71), 0),
        "far_list": draw_far_list(jax.random.fold_in(keys[6], 71), 0),
        "coarse_list": draw_coarse_list(jax.random.fold_in(keys[6], 71), 0),
    }


LENGTH_SCALE = 2.5
AMPLITUDE = 0.025
SHORT_SCALE = 0.5
SHORT_WEIGHT = 0.1
NUGGET = 0.5
LEAF_HALF = 0.75
PARENT_HALF = 1.25


def node_set(node_count):
    node_index = jnp.arange(node_count, dtype=jnp.float32)
    return jnp.cos((2.0 * node_index + 1.0) * (math.pi / (2.0 * node_count)))


def lagrange(values, nodes_used):
    node_count = nodes_used.shape[0]
    columns = []
    for first_node in range(node_count):
        column = jnp.ones_like(values)
        for second in range(node_count):
            if second != first_node:
                column = column * (values - nodes_used[second]) / (nodes_used[first_node] - nodes_used[second])
        columns.append(column)
    return jnp.stack(columns, axis=-1)


def tensor_cube(factor):
    rank_size = factor.shape[1] ** 3
    count_total = factor.shape[0]
    along_x = factor[:, None, None, :, None, None, :, None, None]
    along_y = factor[None, :, None, None, :, None, None, :, None]
    along_z = factor[None, None, :, None, None, :, None, None, :]
    return (along_x * along_y * along_z).reshape(count_total, count_total, count_total, rank_size, rank_size)


def coupling_table(node_count, half_width, cell_width, reach):
    nodes_used = node_set(node_count)
    offsets = jnp.arange(-reach, reach + 1).astype(jnp.float32) * cell_width
    gap_value = half_width * nodes_used[None, :, None] - half_width * nodes_used[None, None, :] - offsets[:, None, None]
    gap_square = gap_value * gap_value
    factor_long = jnp.exp(-gap_square / (LENGTH_SCALE * LENGTH_SCALE))
    factor_short = jnp.exp(-gap_square / (SHORT_SCALE * SHORT_SCALE))
    return (AMPLITUDE * tensor_cube(factor_long) + SHORT_WEIGHT * tensor_cube(factor_short)).astype(jnp.bfloat16)


def transfer_table(node_count):
    nodes_used = node_set(node_count)
    shifts = jnp.array([-0.5, 0.5], dtype=jnp.float32)
    inner_points = (shifts[:, None] + LEAF_HALF * nodes_used[None, :]) / PARENT_HALF
    return tensor_cube(lagrange(inner_points, nodes_used))


def leaf_basis(points, first_x, first_y, node_count):
    nodes_used = node_set(node_count)
    centre_x = (first_x + jnp.arange(points.shape[1], dtype=jnp.int32)).astype(jnp.float32) + 0.5
    centre_y = (first_y + jnp.arange(points.shape[2], dtype=jnp.int32)).astype(jnp.float32) + 0.5
    centre_z = jnp.arange(points.shape[3], dtype=jnp.int32).astype(jnp.float32) + 0.5
    poly_x = lagrange((points[0] - centre_x[:, None, None, None]) / LEAF_HALF, nodes_used)
    poly_y = lagrange((points[1] - centre_y[None, :, None, None]) / LEAF_HALF, nodes_used)
    poly_z = lagrange((points[2] - centre_z[None, None, :, None]) / LEAF_HALF, nodes_used)
    product = poly_x[..., :, None, None] * poly_y[..., None, :, None] * poly_z[..., None, None, :]
    return product.reshape(points.shape[1:] + (node_count ** 3,))


def offset_slots(lists, first_x, first_y, total_y, total_z, reach):
    pos_x = first_x + jnp.arange(lists.shape[1], dtype=jnp.int32)
    pos_y = first_y + jnp.arange(lists.shape[2], dtype=jnp.int32)
    pos_z = jnp.arange(lists.shape[3], dtype=jnp.int32)
    is_valid = lists >= 0
    entry_id = jnp.where(is_valid, lists, 0)
    delta_x = entry_id // (total_y * total_z) - pos_x[None, :, None, None]
    delta_y = (entry_id // total_z) % total_y - pos_y[None, None, :, None]
    delta_z = entry_id % total_z - pos_z[None, None, None, :]
    span_size = 2 * reach + 1
    slot_id = (delta_x + reach) * span_size * span_size + (delta_y + reach) * span_size + delta_z + reach
    return jnp.where(is_valid, slot_id, -1).astype(jnp.int32)


def offset_counts(slots, reach):
    cube_size = (2 * reach + 1) ** 3
    ident_list = jnp.arange(cube_size, dtype=jnp.int32).reshape(cube_size, 1, 1, 1)

    def accumulate(running, slot_row):
        return running + (slot_row[None] == ident_list).astype(jnp.float32), None

    running, _ = lax.scan(accumulate, jnp.zeros((cube_size,) + slots.shape[1:], jnp.float32), slots)
    return running


def settle(value):
    return lax.optimization_barrier(value.astype(jnp.bfloat16)).astype(jnp.float32)


def couple(moments_wide, counts, coupling, reach):
    span_size = 2 * reach + 1
    rank_size = moments_wide.shape[3]
    window_shape = moments_wide.shape
    padded_base = jnp.pad(moments_wide, ((reach, reach), (reach, reach), (reach, reach), (0, 0), (0, 0)))
    flat_table = coupling.reshape(span_size ** 3, rank_size, rank_size)
    zero_index = jnp.zeros((), jnp.int32)

    def accumulate(running, offset_index):
        shift_x = offset_index // (span_size * span_size)
        shift_y = (offset_index // span_size) % span_size
        shift_z = offset_index % span_size
        window = lax.dynamic_slice(padded_base, (shift_x, shift_y, shift_z, zero_index, zero_index), window_shape)
        weight = lax.dynamic_index_in_dim(counts, offset_index, 0, keepdims=False)
        coupling_block = lax.dynamic_index_in_dim(flat_table, offset_index, 0, keepdims=False)
        masked = window * weight[..., None, None]
        return running + jnp.einsum('rq,xyzqs->xyzrs', coupling_block, masked, precision=lax.Precision.HIGHEST), None

    running, _ = lax.scan(accumulate, jnp.zeros(window_shape, jnp.float32), jnp.arange(span_size ** 3, dtype=jnp.int32))
    return running


def reference(coords, charges, leaf_order, near_list, far_list, coarse_list):
    count_x = LX // BX
    count_y = LY // BY
    row_width = LZ * LEAF_PTS
    rank_size = ORDER ** 3

    def to_blocks(array):
        chans = array.shape[0]
        return array.reshape(chans, count_x, BX, count_y, BY, row_width).transpose(1, 3, 0, 2, 4, 5).reshape(count_x, count_y, chans, BX * BY * row_width)

    def from_blocks(blocks):
        chans = blocks.shape[2]
        return blocks.reshape(count_x, count_y, chans, BX, BY, row_width).transpose(2, 0, 3, 1, 4, 5).reshape(chans, LX, LY, row_width)

    order_blocks = to_blocks(leaf_order[None])

    def into_leaf_order(array):
        blocks = to_blocks(array)
        return from_blocks(jnp.take_along_axis(blocks, jnp.broadcast_to(order_blocks, blocks.shape), axis=3))

    points = into_leaf_order(coords).reshape(3, LX, LY, LZ, LEAF_PTS)
    charge_sorted = into_leaf_order(charges).reshape(RHS, LX, LY, LZ, LEAF_PTS)
    charge_wide = settle(charge_sorted)
    firsts = jnp.arange(count_x, dtype=jnp.int32) * BX

    def moment_block(first_row):
        block_points = lax.dynamic_slice_in_dim(points, first_row, BX, 1)
        block_charge = lax.dynamic_slice_in_dim(charge_wide, first_row, BX, 1)
        basis_values = leaf_basis(block_points, first_row, 0, ORDER)
        return jnp.einsum('xyzpr,sxyzp->xyzrs', basis_values, block_charge, precision=lax.Precision.HIGHEST)

    box_moment = lax.map(moment_block, firsts).reshape(LX, LY, LZ, rank_size, RHS)
    moment_wide = settle(box_moment)
    transfer = transfer_table(ORDER)
    grouped = moment_wide.reshape(PX, 2, PY, 2, PZ, 2, rank_size, RHS)
    parent_moment = jnp.einsum('ijkqr,xiyjzkqs->xyzrs', transfer, grouped, precision=lax.Precision.HIGHEST)
    parent_wide = settle(parent_moment)

    leaf_table = settle(coupling_table(ORDER, LEAF_HALF, 1.0, 3))
    parent_table = settle(coupling_table(ORDER, PARENT_HALF, 2.0, 2))
    far_counts = offset_counts(offset_slots(far_list, 0, 0, LY, LZ, 3), 3)
    coarse_counts = offset_counts(offset_slots(coarse_list, 0, 0, PY, PZ, 2), 2)
    box_local = couple(moment_wide, far_counts, leaf_table, 3)
    parent_local = couple(parent_wide, coarse_counts, parent_table, 2)
    descent = jnp.einsum('ijkqr,xyzrs->xiyjzkqs', transfer, parent_local, precision=lax.Precision.HIGHEST)
    local_total = box_local + descent.reshape(LX, LY, LZ, rank_size, RHS)

    near_counts = offset_counts(offset_slots(near_list, 0, 0, LY, LZ, 1), 1)
    stacked = jnp.concatenate([points, charge_wide], axis=0)
    padded = jnp.pad(stacked, ((0, 0), (1, 1), (1, 1), (1, 1), (0, 0)))
    zero_index = jnp.zeros((), jnp.int32)

    def near_block(first_row):
        targets = lax.dynamic_slice_in_dim(points, first_row, BX, 1)
        region = lax.dynamic_slice_in_dim(padded, first_row, BX + 2, 1)
        block_mask = lax.dynamic_slice_in_dim(near_counts, first_row, BX, 1)

        def accumulate(running, offset_index):
            shift_x = offset_index // 9
            shift_y = (offset_index // 3) % 3
            shift_z = offset_index % 3
            window = lax.dynamic_slice(region, (zero_index, shift_x, shift_y, shift_z, zero_index), (3 + RHS, BX, LY, LZ, LEAF_PTS))
            weight = lax.dynamic_index_in_dim(block_mask, offset_index, 0, keepdims=False)
            gap_x = targets[0][..., :, None] - window[0][..., None, :]
            gap_y = targets[1][..., :, None] - window[1][..., None, :]
            gap_z = targets[2][..., :, None] - window[2][..., None, :]
            dist = gap_x * gap_x + gap_y * gap_y + gap_z * gap_z
            values = AMPLITUDE * jnp.exp(-dist / (LENGTH_SCALE * LENGTH_SCALE)) + SHORT_WEIGHT * jnp.exp(-dist / (SHORT_SCALE * SHORT_SCALE))
            kernel = settle(values * weight[..., None, None])
            return running + jnp.einsum('xyzpq,sxyzq->sxyzp', kernel, window[3:], precision=lax.Precision.HIGHEST), None

        running, _ = lax.scan(accumulate, jnp.zeros((RHS, BX, LY, LZ, LEAF_PTS), jnp.float32), jnp.arange(27, dtype=jnp.int32))
        return running

    near_rows = lax.map(near_block, firsts)
    near_field = near_rows.transpose(1, 0, 2, 3, 4, 5).reshape(RHS, LX, LY, LZ, LEAF_PTS)

    def far_block(first_row):
        block_points = lax.dynamic_slice_in_dim(points, first_row, BX, 1)
        block_local = lax.dynamic_slice_in_dim(local_total, first_row, BX, 0)
        basis_values = leaf_basis(block_points, first_row, 0, ORDER)
        return jnp.einsum('xyzpr,xyzrs->sxyzp', basis_values, block_local, precision=lax.Precision.HIGHEST)

    far_rows = lax.map(far_block, firsts)
    far_field = far_rows.transpose(1, 0, 2, 3, 4, 5).reshape(RHS, LX, LY, LZ, LEAF_PTS)
    potential = NUGGET * charge_sorted + near_field + far_field
    return potential.reshape(RHS, LX, LY, row_width)
```

```python
import functools
import math

import jax
import jax.numpy as jnp
import ml_dtypes
import numpy as np
from jax import lax
from jax.experimental import pallas as pl
from jax.experimental.pallas import tpu as pltpu
from jax.sharding import PartitionSpec as P

MESH = pl.DeviceIdType.MESH
BF = jnp.bfloat16
F32 = jnp.float32

ORDER = 4
LENGTH_SCALE = 2.5
AMPLITUDE = 0.025
SHORT_SCALE = 0.5
SHORT_WEIGHT = 0.1
NUGGET = 0.5
LEAF_HALF = 0.75
PARENT_HALF = 1.25

B = 4
PTS = 32
WIDTH = B * PTS
RHS = 8
RANK = ORDER**3

KAPPA = math.log2(math.e) / LENGTH_SCALE**2
SCALE = math.sqrt(2.0 * KAPPA)
RATIO = (LENGTH_SCALE / SHORT_SCALE) ** 2
LOG_LONG = math.log2(AMPLITUDE)
LOG_SHORT = math.log2(SHORT_WEIGHT)
PENALTY = -1024.0

NODES = np.cos((2.0 * np.arange(ORDER) + 1.0) * (math.pi / (2.0 * ORDER)))
NEIGHBOURS = [(i, j) for i in (-1, 0, 1) for j in (-1, 0, 1) if (i, j) != (0, 0)]


def lagrange_np(values):
    out = []
    for a in range(ORDER):
        col = np.ones_like(values)
        for b in range(ORDER):
            if b != a:
                col = col * (values - NODES[b]) / (NODES[a] - NODES[b])
        out.append(col)
    return np.stack(out, axis=-1)


def coupling_np(half, cell, reach):
    offsets = np.arange(-reach, reach + 1) * cell
    gap = half * NODES[None, :, None] - half * NODES[None, None, :] - offsets[:, None, None]
    total = 0.0
    for amp, scale in ((AMPLITUDE, LENGTH_SCALE), (SHORT_WEIGHT, SHORT_SCALE)):
        f = np.exp(-gap * gap / scale**2)
        total = total + amp * np.einsum("xad,ybe,zcf->xyzabcdef", f, f, f)
    n = 2 * reach + 1
    return total.reshape(n, n, n, RANK, RANK)


def leaf_weights():
    table = coupling_np(LEAF_HALF, 1.0, 3)
    w = np.zeros((49, B, RANK, B, RANK))
    for zs in range(B):
        for zt in range(B):
            w[:, zs, :, zt, :] = table[:, :, zs - zt + 3].reshape(49, RANK, RANK).transpose(0, 2, 1)
    return w.reshape(49 * B * RANK, B * RANK).astype(ml_dtypes.bfloat16)


def parent_weights():
    table = coupling_np(PARENT_HALF, 2.0, 2)
    w = np.zeros((26, 2, RANK, 2, RANK))
    for zs in range(2):
        for zt in range(2):
            w[:25, zs, :, zt, :] = table[:, :, zs - zt + 2].reshape(25, RANK, RANK).transpose(0, 2, 1)
    return w.reshape(26 * 2 * RANK, 2 * RANK).astype(ml_dtypes.bfloat16)


def transfer_weights():
    shifts = np.array([-0.5, 0.5])
    f = lagrange_np((shifts[:, None] + LEAF_HALF * NODES[None, :]) / PARENT_HALF)
    t = np.einsum("xad,ybe,zcf->xyzabcdef", f, f, f).reshape(2, 2, 2, RANK, RANK)
    up = np.zeros((2, 2, B, RANK, 2, RANK))
    for z in range(B):
        up[:, :, z, :, z // 2, :] = t[:, :, z % 2]
    up = up.reshape(4, B * RANK, 2 * RANK)
    return (
        up.reshape(4 * B * RANK, 2 * RANK).astype(ml_dtypes.bfloat16),
        up.transpose(2, 0, 1).reshape(2 * RANK, 4 * B * RANK).astype(ml_dtypes.bfloat16),
    )


def iota(shape, dim):
    return lax.broadcasted_iota(jnp.int32, shape, dim)


def dot_nt(a, b):
    return lax.dot_general(a, b, (((1,), (1,)), ((), ())), preferred_element_type=F32)


def split2(v):
    hi = v.astype(BF).astype(F32)
    return hi, (v - hi).astype(BF).astype(F32)


def prep_kernel(coords_ref, charges_ref, order_ref, up_ref, cs_ref, np_ref, mb_ref, pm_ref, bb_ref):
    gx = lax.axis_index("group")
    gy = lax.axis_index("dev")
    cen_x = (B * gx + 2).astype(F32)
    cen_y = (B * gy + 2).astype(F32)
    row8 = iota((8, WIDTH), 0)
    lane8 = iota((8, WIDTH), 1)
    lane_box = lane8 // PTS
    centre = jnp.where(row8 == 0, cen_x, jnp.where(row8 == 1, cen_y, 2.0))
    sources = []
    for c in range(16):
        q = charges_ref[:, c // B, c % B, :]
        xyz = coords_ref[:, c // B, c % B, :]
        xyz = jnp.concatenate([xyz, jnp.zeros((5, WIDTH), F32)], axis=0) - jnp.where(
            row8 < 3, centre, 0.0
        )
        sources.append((q, xyz))
    moments = []
    for c in range(16):
        x, y = c // B, c % B
        order = jnp.broadcast_to(order_ref[x, y : y + 1, :], (8, WIDTH))
        hi = order // WIDTH
        lo = order % WIDTH
        q = jnp.zeros((8, WIDTH), F32)
        xyz = jnp.zeros((8, WIDTH), F32)
        for k in range(16):
            here = hi == k
            q = jnp.where(here, jnp.take_along_axis(sources[k][0], lo, axis=1), q)
            xyz = jnp.where(here, jnp.take_along_axis(sources[k][1], lo, axis=1), xyz)
        cs_ref[c] = q
        q_low = q.astype(BF)
        hi2, lo2 = split2(xyz * SCALE)
        lo3 = jnp.concatenate([jnp.zeros((3, WIDTH), F32), lo2[0:5]], axis=0)
        feat = jnp.where(row8 < 3, hi2, lo3)
        np_ref[x, y] = jnp.concatenate([feat, q_low.astype(F32)], axis=0).astype(BF)

        box_centre = jnp.where(
            row8 == 0, x - 1.5, jnp.where(row8 == 1, y - 1.5, lane_box.astype(F32) - 1.5)
        )
        u = (xyz - box_centre) * (1.0 / LEAF_HALF)
        diffs = [u - float(NODES[k]) for k in range(ORDER)]
        polys = []
        for a in range(ORDER):
            denom = 1.0
            poly = None
            for b in range(ORDER):
                if b != a:
                    denom *= float(NODES[a] - NODES[b])
                    poly = diffs[b] if poly is None else poly * diffs[b]
            polys.append(poly * (1.0 / denom))

        def spread(k, d):
            return jnp.broadcast_to(polys[k][d : d + 1, :], (8, WIDTH))

        r4 = row8 % 4
        z8 = jnp.where(
            r4 < 2,
            jnp.where(r4 == 0, spread(0, 2), spread(1, 2)),
            jnp.where(r4 == 2, spread(2, 2), spread(3, 2)),
        )
        yz = [jnp.where(row8 < 4, spread(2 * j, 1), spread(2 * j + 1, 1)) * z8 for j in range(2)]
        basis = jnp.concatenate([spread(a, 0) * yz[j] for a in range(ORDER) for j in range(2)], axis=0)
        lane64 = iota((RANK, WIDTH), 1) // PTS
        wide = jnp.concatenate([jnp.where(lane64 == z, basis, 0.0) for z in range(B)], axis=0).astype(BF)
        bb_ref[c] = wide
        m = dot_nt(q_low, wide).astype(BF)
        moments.append(m)
        m32 = m.astype(F32)
        mb_ref[x, y] = jnp.concatenate([m32[:, :128], m32[:, 128:]], axis=0).astype(BF)
    for px in range(2):
        rows = []
        for py in range(2):
            kids = [moments[(2 * px + sx) * B + 2 * py + sy].astype(F32) for sx in range(2) for sy in range(2)]
            rows.append(jnp.concatenate(kids, axis=1))
        lhs = jnp.concatenate(rows, axis=0).astype(BF)
        pm_ref[px] = jnp.dot(lhs, up_ref[...], preferred_element_type=F32).astype(BF)


def cut(side, size, width):
    if side == 0:
        return slice(0, size), slice(width, width + size)
    if side > 0:
        return slice(size - width, size), slice(0, width)
    return slice(0, width), slice(width + size, 2 * width + size)


def exchange_kernel(count_g, count_d, np_in, mb_in, pm_in, np_out, mb_out, pm_out, send, recv, local):
    g = lax.axis_index("group")
    d = lax.axis_index("dev")

    def there(i, j):
        return (lax.rem(g + i + count_g, count_g), lax.rem(d + j + count_d, count_d))

    barrier = pltpu.get_barrier_semaphore()
    for i, j in NEIGHBOURS:
        pl.semaphore_signal(barrier, inc=1, device_id=there(i, j), device_id_type=MESH)
    pl.semaphore_wait(barrier, len(NEIGHBOURS))

    def ds(s):
        return pl.ds(s.start, s.stop - s.start)

    copies = []
    for n, (i, j) in enumerate(NEIGHBOURS):
        for k, (src, dst, width) in enumerate(((mb_in, mb_out, 3), (np_in, np_out, 1))):
            sx, dx = cut(i, B, width)
            sy, dy = cut(j, B, width)
            copies.append(
                pltpu.make_async_remote_copy(
                    src_ref=src.at[ds(sx), ds(sy)],
                    dst_ref=dst.at[ds(dx), ds(dy)],
                    send_sem=send.at[n, k],
                    recv_sem=recv.at[n, k],
                    device_id=there(i, j),
                    device_id_type=MESH,
                )
            )
        copies.append(
            pltpu.make_async_remote_copy(
                src_ref=pm_in,
                dst_ref=pm_out.at[pl.ds(2 * (1 - i), 2), 1 - j],
                send_sem=send.at[n, 2],
                recv_sem=recv.at[n, 2],
                device_id=there(i, j),
                device_id_type=MESH,
            )
        )
    for c in copies:
        c.start()
    own = [
        pltpu.make_async_copy(mb_in, mb_out.at[pl.ds(3, B), pl.ds(3, B)], local.at[0]),
        pltpu.make_async_copy(np_in, np_out.at[pl.ds(1, B), pl.ds(1, B)], local.at[1]),
        pltpu.make_async_copy(pm_in, pm_out.at[pl.ds(2, 2), 1], local.at[2]),
    ]
    for c in own:
        c.start()
    for c in own:
        c.wait()
    for c in copies:
        c.wait()


def decode(entries, log_y, first_x, first_y, reach, log_z):
    x = (entries >> (log_y + log_z)) - first_x + reach
    y = ((entries >> log_z) & ((1 << log_y) - 1)) - first_y + reach
    return x * (2 * reach + 1) + y, entries & ((1 << log_z) - 1)


def near_kernel(log_y, list_ref, cs_ref, np_ref, out_ref):
    gx = lax.axis_index("group")
    gy = lax.axis_index("dev")
    row8 = iota((8, WIDTH), 0)
    lane8 = iota((8, WIDTH), 1)
    lane_box = lane8 // PTS
    cols = {}
    for x in range(6):
        for y in range(6):
            tile = np_ref[x, y].astype(F32)
            feat, charge = tile[0:8], tile[8:16]
            lo = jnp.concatenate([feat[3:6], jnp.zeros((5, WIDTH), F32)], axis=0)
            pos = jnp.where(row8 < 3, feat + lo, 0.0)
            sx = B * SCALE * ((x == 5) - (x == 0))
            sy = B * SCALE * ((y == 5) - (y == 0))
            if sx or sy:
                pos = pos + jnp.where(row8 == 0, sx, jnp.where(row8 == 1, sy, 0.0))
            hi, lo = split2(pos)
            tight = hi + lo
            norm = -0.5 * jnp.sum(tight * tight, axis=0, keepdims=True)
            cols[x, y] = (hi, lo, norm, charge.astype(BF))

    def three(v):
        h, l = split2(v)
        return h, l, (v - h - l).astype(BF).astype(F32)

    def spread(v):
        return jnp.broadcast_to(v, (8, WIDTH))

    def twice(v):
        return jnp.where(row8 < 3, v, jnp.concatenate([v[5:8], v[0:5]], axis=0))

    src = {}
    for key, (hi, lo, norm, charge) in cols.items():
        nh, nm, nl = (spread(v) for v in three(norm))
        s0 = jnp.where(row8 < 6, twice(hi), jnp.where(row8 == 6, nh, nm))
        s1 = jnp.where(row8 < 6, twice(lo), jnp.where(row8 == 6, nl, 1.0))
        src[key] = (s0, s1, charge)
    ones2 = jnp.where(row8 < 2, 1.0, 0.0)
    eye = (iota((WIDTH, WIDTH), 0) == iota((WIDTH, WIDTH), 1)).astype(BF)
    outs = []
    for c in range(16):
        x, y = c // B, c % B
        hi, lo, norm, _ = cols[x + 1, y + 1]
        nh, nm, nl = (spread(v) for v in three(norm + LOG_LONG))
        a = jnp.where(row8 < 3, hi, jnp.concatenate([lo[5:8], lo[0:5]], axis=0))
        t0 = jnp.where(row8 < 6, a, 1.0)
        t1 = jnp.where(row8 < 6, a, jnp.where(row8 == 6, 1.0, nh))
        t2 = jnp.where(
            row8 < 4,
            jnp.where(row8 == 0, nm, jnp.where(row8 == 1, nl, 0.0)),
            jnp.where(lane_box == row8 - 4, 1.0, 0.0),
        )
        target = jnp.concatenate([t0, t1, t2, jnp.zeros((8, WIDTH), F32)], axis=0).astype(BF)
        target = dot_nt(eye, target).astype(BF)

        entries = list_ref[x, y]
        slot, zs = decode(entries, log_y, B * gx + x, B * gy + y, 1, 2)
        bit = jnp.where(entries >= 0, jnp.int32(1) << jnp.clip(slot + 9 * (zs & 1), 0, 30), 0)
        w0 = jnp.sum(jnp.where(zs < 2, bit, 0), axis=1, keepdims=True)
        w1 = jnp.sum(jnp.where(zs >= 2, bit, 0), axis=1, keepdims=True)
        w0 = jnp.broadcast_to(jnp.concatenate([w0, w0], axis=0), (8, WIDTH))
        w1 = jnp.broadcast_to(jnp.concatenate([w1, w1], axis=0), (8, WIDTH))
        word = jnp.where(lane_box < 2, w0, w1)
        word = jnp.where(lane_box % 2 == 1, word >> 9, word)
        acc = jnp.zeros((WIDTH, RHS), F32)
        for dx in range(3):
            rhs, charge = [], []
            for dy in range(3):
                k = dx * 3 + dy
                pen = jnp.where((word & (1 << k)) != 0, 0.0, PENALTY)
                s0, s1, q = src[x + dx, y + dy]
                s2 = jnp.where(row8 < 4, ones2, pen)
                rhs.append(jnp.concatenate([s0, s1, s2, jnp.zeros((8, WIDTH), F32)], axis=0).astype(BF))
                charge.append(q)
            u = jnp.dot(target, jnp.concatenate(rhs, axis=1), preferred_element_type=F32)
            v = u * RATIO + (LOG_SHORT - RATIO * LOG_LONG)
            kernel = (jnp.exp2(u) + jnp.exp2(v)).astype(BF)
            acc = acc + dot_nt(kernel, jnp.concatenate(charge, axis=1))
        outs.append(acc)
    turned = jnp.concatenate(outs, axis=1).T
    for c in range(16):
        out_ref[c] = turned[8 * c : 8 * c + 8] + NUGGET * cs_ref[c]


def far_kernel(
    log_y, far_ref, coarse_ref, near_ref, mb_ref, pm_ref, bb_ref, wl_ref, wp_ref, down_ref, out_ref, win, lhs, words
):
    gx = lax.axis_index("group")
    gy = lax.axis_index("dev")
    row8 = iota((8, 128), 0)
    lane4 = iota((4, 128), 1)
    row16 = iota((16, 128), 0)

    def fill(x, carry):
        for y in range(10):
            tile = mb_ref[x, y].astype(F32)
            for half in range(2):
                m = tile[8 * half : 8 * half + 8]
                turned = jnp.concatenate([m[4:8], m[0:4]], axis=0)
                first = jnp.where(row8 < 4, m, turned)
                last = jnp.where(row8 < 4, turned, m)
                win[x, y, 0, :, 128 * half : 128 * half + 128] = jnp.concatenate([first, first], axis=0).astype(BF)
                win[x, y, 1, :, 128 * half : 128 * half + 128] = jnp.concatenate([last, last], axis=0).astype(BF)
        return carry

    lax.fori_loop(0, 10, fill, 0)

    for c in range(16):
        x, y = c // B, c % B
        entries = far_ref[x, y]
        slot, zs = decode(entries, log_y, B * gx + x, B * gy + y, 3, 2)
        late = slot >= 25
        bit = jnp.where(entries >= 0, jnp.int32(1) << jnp.clip(jnp.where(late, slot - 25, slot), 0, 30), 0)
        for h in range(2):
            mine = jnp.where(late == (h == 1), bit, 0)
            w = [jnp.sum(jnp.where(zs == z, mine, 0), axis=1, keepdims=True) for z in range(B)]
            for half in range(2):
                pair = jnp.where(
                    lane4 < 64,
                    jnp.broadcast_to(w[2 * half], (4, 128)),
                    jnp.broadcast_to(w[2 * half + 1], (4, 128)),
                )
                wide = jnp.broadcast_to(pair[0:1], (16, 128))
                for z in range(1, B):
                    wide = jnp.where(row16 >= 4 * z, jnp.broadcast_to(pair[z : z + 1], (16, 128)), wide)
                words[h, c, :, 128 * half : 128 * half + 128] = wide

    for dx in range(7):
        for dy in range(7):
            k = dx * 7 + dy
            h, bit = (0, k) if k < 25 else (1, k - 25)

            def mask_rows(x, carry, dx=dx, dy=dy, k=k, h=h, bit=bit):
                for y in range(B):
                    c = x * B + y
                    keep = jnp.where((words[h, c] & (1 << bit)) != 0, 1.0, 0.0).astype(BF)
                    for s in range(2):
                        r = pl.multiple_of(c * 32 + 16 * s, 16)
                        lhs[pl.ds(r, 16), 256 * k : 256 * k + 256] = keep * win[x + dx, y + dy, s]
                return carry

            lax.fori_loop(0, B, mask_rows, 0, unroll=True)
    local = jnp.dot(lhs[...], wl_ref[...], preferred_element_type=F32)

    row16p = iota((16, 128), 0)
    lane2 = iota((2, 128), 1)
    rows = []
    for px in range(2):
        for py in range(2):
            entries = coarse_ref[px, py]
            slot, zs = decode(entries, log_y - 1, 2 * gx + px, 2 * gy + py, 2, 1)
            bit = jnp.where(entries >= 0, jnp.int32(1) << jnp.clip(slot, 0, 30), 0)
            w = [jnp.sum(jnp.where(zs == z, bit, 0), axis=1, keepdims=True) for z in range(2)]
            pair = jnp.where(
                lane2 < 64, jnp.broadcast_to(w[0], (2, 128)), jnp.broadcast_to(w[1], (2, 128))
            )
            wide = jnp.where(
                row16p < 8, jnp.broadcast_to(pair[0:1], (16, 128)), jnp.broadcast_to(pair[1:2], (16, 128))
            )
            parts = []
            for dx in range(5):
                for dy in range(5):
                    k = dx * 5 + dy
                    tile = pm_ref[px + dx, (py + dy) // 2].astype(F32)
                    r = 8 * ((py + dy) % 2)
                    m = tile[r : r + 8]
                    m = jnp.concatenate([m, m], axis=0)
                    parts.append(jnp.where((wide & (1 << k)) != 0, m, 0.0))
            parts.append(jnp.zeros((16, 128), F32))
            rows.append(jnp.concatenate(parts, axis=1).astype(BF))
    parent = jnp.dot(jnp.concatenate(rows, axis=0), wp_ref[...], preferred_element_type=F32)
    lane8 = iota((8, 128), 1)
    picked = jnp.concatenate(
        [jnp.where(lane8 < 64, parent[16 * q : 16 * q + 8], parent[16 * q + 8 : 16 * q + 16]) for q in range(4)],
        axis=0,
    ).astype(BF)
    descent = jnp.dot(picked, down_ref[...], preferred_element_type=F32)

    lane_z = iota((4, 256), 1) // RANK
    for c in range(16):
        x, y = c // B, c % B
        halves = []
        for s in range(2):
            block = local[c * 32 + 16 * s : c * 32 + 16 * s + 16]
            got = block[0:4]
            for z in range(1, B):
                got = jnp.where(lane_z == z, block[4 * z : 4 * z + 4], got)
            halves.append(got)
        q = (x // 2) * 2 + y // 2
        k = (x % 2) * 2 + y % 2
        total = jnp.concatenate(halves, axis=0) + descent[8 * q : 8 * q + 8, 256 * k : 256 * k + 256]
        far = jnp.dot(total.astype(BF), bb_ref[c], preferred_element_type=F32)
        out_ref[:, x, y, :] = near_ref[c] + far


def vmem(n):
    return [pl.BlockSpec(memory_space=pltpu.VMEM)] * n


def params(mib, **kw):
    return pltpu.CompilerParams(vmem_limit_bytes=mib << 20, **kw)


def on_device(count_g, count_d, wl, wp, up, down, coords, charges, order, near_list, far_list, coarse_list):
    log_y = (count_d * B).bit_length() - 1
    sds = jax.ShapeDtypeStruct
    cs, near_pay, moments, parents, basis = pl.pallas_call(
        prep_kernel,
        out_shape=(
            sds((16, RHS, WIDTH), F32),
            sds((B, B, 16, WIDTH), BF),
            sds((B, B, 16, 128), BF),
            sds((2, 16, 128), BF),
            sds((16, B * RANK, WIDTH), BF),
        ),
        in_specs=vmem(4),
        out_specs=tuple(vmem(5)),
        compiler_params=params(32),
        name="prep",
    )(coords, charges, order, up)
    near_halo, moment_halo, parent_halo = pl.pallas_call(
        functools.partial(exchange_kernel, count_g, count_d),
        out_shape=(
            sds((6, 6, 16, WIDTH), BF),
            sds((10, 10, 16, 128), BF),
            sds((6, 3, 16, 128), BF),
        ),
        in_specs=vmem(3),
        out_specs=tuple(vmem(3)),
        scratch_shapes=[
            pltpu.SemaphoreType.DMA((8, 3)),
            pltpu.SemaphoreType.DMA((8, 3)),
            pltpu.SemaphoreType.DMA((3,)),
        ],
        compiler_params=params(16, collective_id=0, has_side_effects=True),
        name="exchange",
    )(near_pay, moments, parents)
    near = pl.pallas_call(
        functools.partial(near_kernel, log_y),
        out_shape=sds((16, RHS, WIDTH), F32),
        in_specs=vmem(3),
        out_specs=vmem(1)[0],
        compiler_params=params(32),
        name="near",
    )(near_list.transpose(1, 2, 3, 0), cs, near_halo)
    return pl.pallas_call(
        functools.partial(far_kernel, log_y),
        out_shape=sds((RHS, B, B, WIDTH), F32),
        in_specs=vmem(9),
        out_specs=vmem(1)[0],
        scratch_shapes=[
            pltpu.VMEM((10, 10, 2, 16, 256), BF),
            pltpu.VMEM((512, 49 * 256), BF),
            pltpu.VMEM((2, 16, 16, 256), jnp.int32),
        ],
        compiler_params=params(48),
        name="far",
    )(
        far_list.transpose(1, 2, 3, 0),
        coarse_list.transpose(1, 2, 3, 0),
        near,
        moment_halo,
        parent_halo,
        basis,
        wl,
        wp,
        down,
    )


def solution(mesh):
    placed = (
        P(None, "group", "dev", None),
        P(None, "group", "dev", None),
        P("group", "dev", None),
        P(None, "group", "dev", None),
        P(None, "group", "dev", None),
        P(None, "group", "dev", None),
    )
    up, down = transfer_weights()
    wl, wp = leaf_weights(), parent_weights()

    def body(*args):
        return on_device(
            mesh.shape["group"],
            mesh.shape["dev"],
            jnp.asarray(wl),
            jnp.asarray(wp),
            jnp.asarray(up),
            jnp.asarray(down),
            *args,
        )

    return jax.shard_map(
        body,
        mesh=mesh,
        in_specs=placed,
        out_specs=P(None, "group", "dev", None),
        check_vma=False,
    )
```

```python
import functools
import math

import jax
import jax.numpy as jnp
import ml_dtypes
import numpy as np
from jax import lax
from jax.experimental import pallas as pl
from jax.experimental.pallas import tpu as pltpu
from jax.sharding import PartitionSpec as P

MESH = pl.DeviceIdType.MESH
BF = jnp.bfloat16
F32 = jnp.float32

ORDER = 4
LENGTH_SCALE = 2.5
AMPLITUDE = 0.025
SHORT_SCALE = 0.5
SHORT_WEIGHT = 0.1
NUGGET = 0.5
LEAF_HALF = 0.75
PARENT_HALF = 1.25

B = 4
PTS = 32
WIDTH = B * PTS
RHS = 8
RANK = ORDER**3

KAPPA = math.log2(math.e) / LENGTH_SCALE**2
SCALE = math.sqrt(2.0 * KAPPA)
RATIO = (LENGTH_SCALE / SHORT_SCALE) ** 2
LOG_LONG = math.log2(AMPLITUDE)
LOG_SHORT = math.log2(SHORT_WEIGHT)
PENALTY = -1024.0

NODES = np.cos((2.0 * np.arange(ORDER) + 1.0) * (math.pi / (2.0 * ORDER)))
NEIGHBOURS = [(i, j) for i in (-1, 0, 1) for j in (-1, 0, 1) if (i, j) != (0, 0)]


def lagrange_np(values):
    out = []
    for a in range(ORDER):
        col = np.ones_like(values)
        for b in range(ORDER):
            if b != a:
                col = col * (values - NODES[b]) / (NODES[a] - NODES[b])
        out.append(col)
    return np.stack(out, axis=-1)


def coupling_np(half, cell, reach):
    offsets = np.arange(-reach, reach + 1) * cell
    gap = half * NODES[None, :, None] - half * NODES[None, None, :] - offsets[:, None, None]
    total = 0.0
    for amp, scale in ((AMPLITUDE, LENGTH_SCALE), (SHORT_WEIGHT, SHORT_SCALE)):
        f = np.exp(-gap * gap / scale**2)
        total = total + amp * np.einsum("xad,ybe,zcf->xyzabcdef", f, f, f)
    n = 2 * reach + 1
    return total.reshape(n, n, n, RANK, RANK)


def leaf_weights():
    table = coupling_np(LEAF_HALF, 1.0, 3)
    w = np.zeros((49, B, RANK, B, RANK))
    for zs in range(B):
        for zt in range(B):
            w[:, zs, :, zt, :] = table[:, :, zs - zt + 3].reshape(49, RANK, RANK).transpose(0, 2, 1)
    return w.reshape(49 * B * RANK, B * RANK).astype(ml_dtypes.bfloat16)


def parent_weights():
    table = coupling_np(PARENT_HALF, 2.0, 2)
    w = np.zeros((26, 2, RANK, 2, RANK))
    for zs in range(2):
        for zt in range(2):
            w[:25, zs, :, zt, :] = table[:, :, zs - zt + 2].reshape(25, RANK, RANK).transpose(0, 2, 1)
    return w.reshape(26 * 2 * RANK, 2 * RANK).astype(ml_dtypes.bfloat16)


def transfer_weights():
    shifts = np.array([-0.5, 0.5])
    f = lagrange_np((shifts[:, None] + LEAF_HALF * NODES[None, :]) / PARENT_HALF)
    t = np.einsum("xad,ybe,zcf->xyzabcdef", f, f, f).reshape(2, 2, 2, RANK, RANK)
    up = np.zeros((2, 2, B, RANK, 2, RANK))
    for z in range(B):
        up[:, :, z, :, z // 2, :] = t[:, :, z % 2]
    up = up.reshape(4, B * RANK, 2 * RANK)
    return (
        up.reshape(4 * B * RANK, 2 * RANK).astype(ml_dtypes.bfloat16),
        up.transpose(2, 0, 1).reshape(2 * RANK, 4 * B * RANK).astype(ml_dtypes.bfloat16),
    )


def iota(shape, dim):
    return lax.broadcasted_iota(jnp.int32, shape, dim)


def dot_nt(a, b):
    return lax.dot_general(a, b, (((1,), (1,)), ((), ())), preferred_element_type=F32)


def split2(v):
    hi = v.astype(BF).astype(F32)
    return hi, (v - hi).astype(BF).astype(F32)


def prepare(gx, gy, coords_ref, charges_ref, order_ref, up_ref, cs_ref, np_ref, mb_ref, pm_ref, bb_ref):
    cen_x = (B * gx + 2).astype(F32)
    cen_y = (B * gy + 2).astype(F32)
    row8 = iota((8, WIDTH), 0)
    lane8 = iota((8, WIDTH), 1)
    lane_box = lane8 // PTS
    centre = jnp.where(row8 == 0, cen_x, jnp.where(row8 == 1, cen_y, 2.0))
    sources = []
    for c in range(16):
        q = charges_ref[:, c // B, c % B, :]
        xyz = coords_ref[:, c // B, c % B, :]
        xyz = jnp.concatenate([xyz, jnp.zeros((5, WIDTH), F32)], axis=0) - jnp.where(
            row8 < 3, centre, 0.0
        )
        sources.append((q, xyz))
    moments = []
    for c in range(16):
        x, y = c // B, c % B
        order = jnp.broadcast_to(order_ref[x, y : y + 1, :], (8, WIDTH))
        hi = order // WIDTH
        lo = order % WIDTH
        q = jnp.zeros((8, WIDTH), F32)
        xyz = jnp.zeros((8, WIDTH), F32)
        for k in range(16):
            here = hi == k
            q = jnp.where(here, jnp.take_along_axis(sources[k][0], lo, axis=1), q)
            xyz = jnp.where(here, jnp.take_along_axis(sources[k][1], lo, axis=1), xyz)
        cs_ref[c] = q
        q_low = q.astype(BF)
        hi2, lo2 = split2(xyz * SCALE)
        lo3 = jnp.concatenate([jnp.zeros((3, WIDTH), F32), lo2[0:5]], axis=0)
        feat = jnp.where(row8 < 3, hi2, lo3)
        np_ref[x, y] = jnp.concatenate([feat, q_low.astype(F32)], axis=0).astype(BF)

        box_centre = jnp.where(
            row8 == 0, x - 1.5, jnp.where(row8 == 1, y - 1.5, lane_box.astype(F32) - 1.5)
        )
        u = (xyz - box_centre) * (1.0 / LEAF_HALF)
        diffs = [u - float(NODES[k]) for k in range(ORDER)]
        polys = []
        for a in range(ORDER):
            denom = 1.0
            poly = None
            for b in range(ORDER):
                if b != a:
                    denom *= float(NODES[a] - NODES[b])
                    poly = diffs[b] if poly is None else poly * diffs[b]
            polys.append(poly * (1.0 / denom))

        def spread(k, d):
            return jnp.broadcast_to(polys[k][d : d + 1, :], (8, WIDTH))

        r4 = row8 % 4
        z8 = jnp.where(
            r4 < 2,
            jnp.where(r4 == 0, spread(0, 2), spread(1, 2)),
            jnp.where(r4 == 2, spread(2, 2), spread(3, 2)),
        )
        yz = [jnp.where(row8 < 4, spread(2 * j, 1), spread(2 * j + 1, 1)) * z8 for j in range(2)]
        basis = jnp.concatenate([spread(a, 0) * yz[j] for a in range(ORDER) for j in range(2)], axis=0)
        lane64 = iota((RANK, WIDTH), 1) // PTS
        wide = jnp.concatenate([jnp.where(lane64 == z, basis, 0.0) for z in range(B)], axis=0).astype(BF)
        bb_ref[c] = wide
        m = dot_nt(q_low, wide).astype(BF)
        moments.append(m)
        m32 = m.astype(F32)
        mb_ref[x, y] = jnp.concatenate([m32[:, :128], m32[:, 128:]], axis=0).astype(BF)
    for px in range(2):
        rows = []
        for py in range(2):
            kids = [moments[(2 * px + sx) * B + 2 * py + sy].astype(F32) for sx in range(2) for sy in range(2)]
            rows.append(jnp.concatenate(kids, axis=1))
        lhs = jnp.concatenate(rows, axis=0).astype(BF)
        pm_ref[px] = jnp.dot(lhs, up_ref[...], preferred_element_type=F32).astype(BF)


def cut(side, size, width):
    if side == 0:
        return pl.ds(0, size), pl.ds(width, size)
    if side > 0:
        return pl.ds(size - width, width), pl.ds(0, width)
    return pl.ds(0, width), pl.ds(width + size, width)


def decode(entries, log_y, first_x, first_y, reach, log_z):
    x = (entries >> (log_y + log_z)) - first_x + reach
    y = ((entries >> log_z) & ((1 << log_y) - 1)) - first_y + reach
    return x, y, entries & ((1 << log_z) - 1)


def one_bit(entries, position):
    return jnp.where(entries >= 0, jnp.int32(1) << jnp.clip(position, 0, 30), 0)


def main_kernel(
    count_g,
    count_d,
    log_y,
    coords_in,
    charges_in,
    order_in,
    near_in,
    far_in,
    coarse_in,
    up_in,
    wl_in,
    wp_in,
    down_in,
    out_ref,
    coords,
    charges,
    order,
    near_list,
    far_list,
    coarse_list,
    up,
    wl,
    wp,
    down,
    cs,
    np_in,
    mb_in,
    pm_in,
    basis,
    near_out,
    np_halo,
    mb_halo,
    pm_halo,
    win,
    lhs,
    words,
    targets,
    near_words,
    load_sem,
    send,
    recv,
):
    g = lax.axis_index("group")
    d = lax.axis_index("dev")

    def there(i, j):
        return (lax.rem(g + i + count_g, count_g), lax.rem(d + j + count_d, count_d))

    loads = [
        pltpu.make_async_copy(src, dst, load_sem.at[n])
        for n, (src, dst) in enumerate(
            (
                (coords_in, coords),
                (charges_in, charges),
                (order_in, order),
                (up_in, up),
                (near_in, near_list),
                (far_in, far_list),
                (coarse_in, coarse_list),
                (wp_in, wp),
                (down_in, down),
                (wl_in, wl),
            )
        )
    ]
    for load in loads:
        load.start()

    barrier = pltpu.get_barrier_semaphore()
    for i, j in NEIGHBOURS:
        pl.semaphore_signal(barrier, inc=1, device_id=there(i, j), device_id_type=MESH)
    for load in loads[:4]:
        load.wait()
    prepare(g, d, coords, charges, order, up, cs, np_in, mb_in, pm_in, basis)
    pl.semaphore_wait(barrier, len(NEIGHBOURS))

    def remote(n, k, src, dst):
        return pltpu.make_async_remote_copy(
            src_ref=src,
            dst_ref=dst,
            send_sem=send.at[n, k],
            recv_sem=recv.at[n, k],
            device_id=there(*NEIGHBOURS[n]),
            device_id_type=MESH,
        )

    near_copies, moment_copies, parent_copies = [], [], []
    for n, (i, j) in enumerate(NEIGHBOURS):
        (sx, tx), (sy, ty) = cut(i, B, 1), cut(j, B, 1)
        near_copies.append(remote(n, 0, np_in.at[sx, sy], np_halo.at[tx, ty]))
        (sx, tx), (sy, ty) = cut(i, B, 3), cut(j, B, 3)
        moment_copies.append(remote(n, 1, mb_in.at[sx, sy], mb_halo.at[tx, ty]))
        parent_copies.append(remote(n, 2, pm_in, pm_halo.at[pl.ds(2 * (1 - i), 2), 1 - j]))
    for copy in near_copies + moment_copies + parent_copies:
        copy.start()

    row8 = iota((8, WIDTH), 0)
    lane8 = iota((8, WIDTH), 1)
    lane_box = lane8 // PTS
    lane4 = iota((4, 128), 1)
    row16 = iota((16, 128), 0)
    zeros8 = jnp.zeros((8, WIDTH), F32)

    def column(tile, sx, sy):
        feat, charge = tile[0:8], tile[8:16]
        lo = jnp.concatenate([feat[3:6], jnp.zeros((5, WIDTH), F32)], axis=0)
        pos = jnp.where(row8 < 3, feat + lo, 0.0)
        if sx or sy:
            pos = pos + jnp.where(row8 == 0, B * SCALE * sx, jnp.where(row8 == 1, B * SCALE * sy, 0.0))
        hi, lo = split2(pos)
        tight = hi + lo
        norm = -0.5 * jnp.sum(tight * tight, axis=0, keepdims=True)
        return hi, lo, norm, charge.astype(BF)

    def three(v):
        h, m = split2(v)
        low = (v - h - m).astype(BF).astype(F32)
        return [jnp.broadcast_to(part, (8, WIDTH)) for part in (h, m, low)]

    def twice(v):
        return jnp.where(row8 < 3, v, jnp.concatenate([v[5:8], v[0:5]], axis=0))

    def source(col):
        hi, lo, norm, charge = col
        nh, nm, nl = three(norm)
        s0 = jnp.where(row8 < 6, twice(hi), jnp.where(row8 == 6, nh, nm))
        s1 = jnp.where(row8 < 6, twice(lo), jnp.where(row8 == 6, nl, 1.0))
        return s0, s1, charge

    ones2 = jnp.where(row8 < 2, 1.0, 0.0)

    def pairs(target, word, sources):
        rhs = []
        for slot, (s0, s1, _) in sources:
            pen = jnp.where((word & (1 << slot)) != 0, 0.0, PENALTY)
            rhs.append(jnp.concatenate([s0, s1, jnp.where(row8 < 4, ones2, pen), zeros8], axis=0).astype(BF))
        u = jnp.dot(target, jnp.concatenate(rhs, axis=1), preferred_element_type=F32)
        kernel = jnp.exp2(u) + jnp.exp2(u * RATIO + (LOG_SHORT - RATIO * LOG_LONG))
        return dot_nt(kernel.astype(BF), jnp.concatenate([s[2] for _, s in sources], axis=1))

    def window(x, y, tile):
        for half in range(2):
            m = tile[8 * half : 8 * half + 8].astype(F32)
            turned = jnp.concatenate([m[4:8], m[0:4]], axis=0)
            first = jnp.where(row8 < 4, m, turned)
            last = jnp.where(row8 < 4, turned, m)
            lanes = slice(128 * half, 128 * half + 128)
            win[x, y, 0, :, lanes] = jnp.concatenate([first, first], axis=0).astype(BF)
            win[x, y, 1, :, lanes] = jnp.concatenate([last, last], axis=0).astype(BF)

    def lhs_at(x, dx, y, dy, s):
        rows = pl.ds(pl.multiple_of(x * 128 + y * 32 + 16 * s, 16), 16)
        return rows, pl.ds(pl.multiple_of(dx * 1792 + 256 * dy, 256), 256)

    def multiply(x, dx, y, dy):
        for s in range(2):
            rows, lanes = lhs_at(x, dx, y, dy, s)
            lhs[rows, lanes] = lhs[rows, lanes] * win[x + dx, y + dy, s]

    def halo_shift(x, t):
        return t + 4 * ((x + t) // 3)

    for load in loads[4:9]:
        load.wait()

    def far_words(x, carry):
        for y in range(B):
            entries = far_list[x, y]
            ox, oy, zs = decode(entries, log_y, B * g + x, B * d + y, 3, 2)
            late = oy >= 4
            bit = one_bit(entries, jnp.where(late, 3 * ox + oy - 4, 4 * ox + oy))
            for h in range(2):
                mine = jnp.where(late == (h == 1), bit, 0)
                w = [jnp.sum(jnp.where(zs == z, mine, 0), axis=1, keepdims=True) for z in range(B)]
                for half in range(2):
                    pair = jnp.where(
                        lane4 < 64,
                        jnp.broadcast_to(w[2 * half], (4, 128)),
                        jnp.broadcast_to(w[2 * half + 1], (4, 128)),
                    )
                    wide = jnp.broadcast_to(pair[0:1], (16, 128))
                    for z in range(1, B):
                        wide = jnp.where(row16 >= 4 * z, jnp.broadcast_to(pair[z : z + 1], (16, 128)), wide)
                    words[h, x, y, :, 128 * half : 128 * half + 128] = wide
        return carry

    lax.fori_loop(0, B, far_words, 0)

    def masks(n, carry):
        x, dx = n // 7, n % 7
        for y in range(B):
            w0 = words[0, x, y] >> (4 * dx)
            w1 = words[1, x, y] >> (3 * dx)
            for dy in range(7):
                w, bit = (w0, dy) if dy < 4 else (w1, dy - 4)
                keep = jnp.where((w & (1 << bit)) != 0, 1.0, 0.0).astype(BF)
                for s in range(2):
                    rows, lanes = lhs_at(x, dx, y, dy, s)
                    lhs[rows, lanes] = keep
        return carry

    lax.fori_loop(0, 28, masks, 0)

    def own_windows(x, carry):
        for y in range(B):
            window(x + 3, y + 3, mb_in[x, y])
        return carry

    lax.fori_loop(0, B, own_windows, 0)

    def own_products(n, carry):
        x = n // 4
        dx = 3 - x + n % 4
        for y in range(B):
            for dy in range(3 - y, 7 - y):
                multiply(x, dx, y, dy)
        return carry

    lax.fori_loop(0, 16, own_products, 0)

    own = {}
    for x in range(B):
        for y in range(B):
            own[x, y] = column(np_in[x, y].astype(F32), 0, 0)
    own_source = {key: source(col) for key, col in own.items()}
    eye = (iota((WIDTH, WIDTH), 0) == iota((WIDTH, WIDTH), 1)).astype(BF)
    outs = []
    for c in range(16):
        x, y = c // B, c % B
        hi, lo, norm, _ = own[x, y]
        nh, nm, nl = three(norm + LOG_LONG)
        a = jnp.where(row8 < 3, hi, jnp.concatenate([lo[5:8], lo[0:5]], axis=0))
        t0 = jnp.where(row8 < 6, a, 1.0)
        t1 = jnp.where(row8 < 6, a, jnp.where(row8 == 6, 1.0, nh))
        t2 = jnp.where(
            row8 < 4,
            jnp.where(row8 == 0, nm, jnp.where(row8 == 1, nl, 0.0)),
            jnp.where(lane_box == row8 - 4, 1.0, 0.0),
        )
        target = dot_nt(eye, jnp.concatenate([t0, t1, t2, zeros8], axis=0).astype(BF)).astype(BF)
        targets[c] = target

        entries = near_list[x, y]
        ox, oy, zs = decode(entries, log_y, B * g + x, B * d + y, 1, 2)
        bit = one_bit(entries, 3 * ox + oy + 9 * (zs & 1))
        w0 = jnp.sum(jnp.where(zs < 2, bit, 0), axis=1, keepdims=True)
        w1 = jnp.sum(jnp.where(zs >= 2, bit, 0), axis=1, keepdims=True)
        w0 = jnp.broadcast_to(jnp.concatenate([w0, w0], axis=0), (8, WIDTH))
        w1 = jnp.broadcast_to(jnp.concatenate([w1, w1], axis=0), (8, WIDTH))
        word = jnp.where(lane_box < 2, w0, w1)
        word = jnp.where(lane_box % 2 == 1, word >> 9, word)
        near_words[c] = word
        acc = jnp.zeros((WIDTH, RHS), F32)
        for dx in (-1, 0, 1):
            sources = [
                (3 * (dx + 1) + dy + 1, own_source[x + dx, y + dy])
                for dy in (-1, 0, 1)
                if (x + dx, y + dy) in own_source
            ]
            if sources:
                acc = acc + pairs(target, word, sources)
        outs.append(acc)
    turned = jnp.concatenate(outs, axis=1).T
    for c in range(16):
        near_out[c] = turned[8 * c : 8 * c + 8]

    pm_halo[pl.ds(2, 2), 1] = pm_in[...]

    for copy in near_copies:
        copy.wait_recv()
    halo_source = {}
    for x in range(6):
        for y in range(6):
            sx, sy = (x == 5) - (x == 0), (y == 5) - (y == 0)
            if sx or sy:
                halo_source[x, y] = source(column(np_halo[x, y].astype(F32), sx, sy))
    outs = []
    for c in range(16):
        x, y = c // B, c % B
        sources = [
            (3 * dx + dy, halo_source[x + dx, y + dy])
            for dx in range(3)
            for dy in range(3)
            if (x + dx, y + dy) in halo_source
        ]
        if sources:
            outs.append(pairs(targets[c], near_words[c], sources))
        else:
            outs.append(jnp.zeros((WIDTH, RHS), F32))
    turned = jnp.concatenate(outs, axis=1).T
    for c in range(16):
        near_out[c] = near_out[c] + turned[8 * c : 8 * c + 8]

    for copy in parent_copies:
        copy.wait_recv()
    lane2 = iota((2, 128), 1)
    rows = []
    for px in range(2):
        for py in range(2):
            entries = coarse_list[px, py]
            ox, oy, zs = decode(entries, log_y - 1, 2 * g + px, 2 * d + py, 2, 1)
            bit = one_bit(entries, 5 * ox + oy)
            w = [jnp.sum(jnp.where(zs == z, bit, 0), axis=1, keepdims=True) for z in range(2)]
            pair = jnp.where(lane2 < 64, jnp.broadcast_to(w[0], (2, 128)), jnp.broadcast_to(w[1], (2, 128)))
            wide = jnp.where(
                row16 < 8, jnp.broadcast_to(pair[0:1], (16, 128)), jnp.broadcast_to(pair[1:2], (16, 128))
            )
            parts = []
            for dx in range(5):
                for dy in range(5):
                    tile = pm_halo[px + dx, (py + dy) // 2].astype(F32)
                    r = 8 * ((py + dy) % 2)
                    m = tile[r : r + 8]
                    m = jnp.concatenate([m, m], axis=0)
                    parts.append(jnp.where((wide & (1 << (5 * dx + dy))) != 0, m, 0.0))
            parts.append(jnp.zeros((16, 128), F32))
            rows.append(jnp.concatenate(parts, axis=1).astype(BF))
    parent = jnp.dot(jnp.concatenate(rows, axis=0), wp[...], preferred_element_type=F32)
    picked = jnp.concatenate(
        [jnp.where(lane8 < 64, parent[16 * q : 16 * q + 8], parent[16 * q + 8 : 16 * q + 16]) for q in range(4)],
        axis=0,
    ).astype(BF)
    descent = jnp.dot(picked, down[...], preferred_element_type=F32)

    for copy in moment_copies:
        copy.wait_recv()
    loads[9].wait()

    def outer_windows(n, carry):
        x = n + 4 * (n // 3)
        for y in range(10):
            window(x, y, mb_halo[x, y])
        return carry

    lax.fori_loop(0, 6, outer_windows, 0)

    def side_windows(x, carry):
        for y in (0, 1, 2, 7, 8, 9):
            window(x, y, mb_halo[x, y])
        return carry

    lax.fori_loop(3, 7, side_windows, 0)

    def outer_products(n, carry):
        x = n // 3
        dx = halo_shift(x, n % 3)
        for y in range(B):
            for dy in range(7):
                multiply(x, dx, y, dy)
        return carry

    lax.fori_loop(0, 12, outer_products, 0)

    def side_products(n, carry):
        x = n // 4
        dx = 3 - x + n % 4
        for y in range(B):
            for t in range(3):
                multiply(x, dx, y, halo_shift(y, t))
        return carry

    lax.fori_loop(0, 16, side_products, 0)
    local = jnp.dot(lhs[...], wl[...], preferred_element_type=F32)

    lane_z = iota((4, 256), 1) // RANK
    for c in range(16):
        x, y = c // B, c % B
        halves = []
        for s in range(2):
            block = local[c * 32 + 16 * s : c * 32 + 16 * s + 16]
            got = block[0:4]
            for z in range(1, B):
                got = jnp.where(lane_z == z, block[4 * z : 4 * z + 4], got)
            halves.append(got)
        q = (x // 2) * 2 + y // 2
        k = (x % 2) * 2 + y % 2
        total = jnp.concatenate(halves, axis=0) + descent[8 * q : 8 * q + 8, 256 * k : 256 * k + 256]
        far = jnp.dot(total.astype(BF), basis[c], preferred_element_type=F32)
        out_ref[:, x, y, :] = NUGGET * cs[c] + near_out[c] + far
    for copy in near_copies + moment_copies + parent_copies:
        copy.wait_send()


def vmem(n):
    return [pl.BlockSpec(memory_space=pltpu.VMEM)] * n


def anywhere(n):
    return [pl.BlockSpec(memory_space=pltpu.HBM)] * n


def params(mib, **kw):
    return pltpu.CompilerParams(vmem_limit_bytes=mib << 20, **kw)


def on_device(count_g, count_d, wl, wp, up, down, coords, charges, order, near_list, far_list, coarse_list):
    log_y = (count_d * B).bit_length() - 1
    near_list = near_list.transpose(1, 2, 3, 0)
    far_list = far_list.transpose(1, 2, 3, 0)
    coarse_list = coarse_list.transpose(1, 2, 3, 0)
    operands = (coords, charges, order, near_list, far_list, coarse_list, up, wl, wp, down)
    return pl.pallas_call(
        functools.partial(main_kernel, count_g, count_d, log_y),
        out_shape=jax.ShapeDtypeStruct((RHS, B, B, WIDTH), F32),
        in_specs=[pl.BlockSpec(memory_space=pl.ANY)] * len(operands),
        out_specs=pl.BlockSpec(memory_space=pltpu.VMEM),
        scratch_shapes=[pltpu.VMEM(a.shape, a.dtype) for a in operands]
        + [
            pltpu.VMEM((16, RHS, WIDTH), F32),
            pltpu.VMEM((B, B, 16, WIDTH), BF),
            pltpu.VMEM((B, B, 16, 128), BF),
            pltpu.VMEM((2, 16, 128), BF),
            pltpu.VMEM((16, B * RANK, WIDTH), BF),
            pltpu.VMEM((16, RHS, WIDTH), F32),
            pltpu.VMEM((6, 6, 16, WIDTH), BF),
            pltpu.VMEM((10, 10, 16, 128), BF),
            pltpu.VMEM((6, 3, 16, 128), BF),
            pltpu.VMEM((10, 10, 2, 16, 256), BF),
            pltpu.VMEM((512, 49 * 256), BF),
            pltpu.VMEM((2, B, B, 16, 256), jnp.int32),
            pltpu.VMEM((16, WIDTH, 32), BF),
            pltpu.VMEM((16, 8, WIDTH), jnp.int32),
            pltpu.SemaphoreType.DMA((len(operands),)),
            pltpu.SemaphoreType.DMA((8, 3)),
            pltpu.SemaphoreType.DMA((8, 3)),
        ],
        compiler_params=pltpu.CompilerParams(
            vmem_limit_bytes=60 << 20, collective_id=0, has_side_effects=True
        ),
        name="fields",
    )(*operands)


def solution(mesh):
    placed = (
        P(None, "group", "dev", None),
        P(None, "group", "dev", None),
        P("group", "dev", None),
        P(None, "group", "dev", None),
        P(None, "group", "dev", None),
        P(None, "group", "dev", None),
    )
    up, down = transfer_weights()
    wl, wp = leaf_weights(), parent_weights()

    def body(*args):
        return on_device(
            mesh.shape["group"],
            mesh.shape["dev"],
            jnp.asarray(wl),
            jnp.asarray(wp),
            jnp.asarray(up),
            jnp.asarray(down),
            *args,
        )

    return jax.shard_map(
        body,
        mesh=mesh,
        in_specs=placed,
        out_specs=P(None, "group", "dev", None),
        check_vma=False,
    )
```

```python
import functools
import math

import jax
import jax.numpy as jnp
import ml_dtypes
import numpy as np
from jax import lax
from jax.experimental import pallas as pl
from jax.experimental.pallas import tpu as pltpu
from jax.sharding import PartitionSpec as P

MESH = pl.DeviceIdType.MESH
BF = jnp.bfloat16
F32 = jnp.float32

ORDER = 4
LENGTH_SCALE = 2.5
AMPLITUDE = 0.025
SHORT_SCALE = 0.5
SHORT_WEIGHT = 0.1
NUGGET = 0.5
LEAF_HALF = 0.75
PARENT_HALF = 1.25

B = 4
PTS = 32
WIDTH = B * PTS
RHS = 8
RANK = ORDER**3

KAPPA = math.log2(math.e) / LENGTH_SCALE**2
SCALE = math.sqrt(2.0 * KAPPA)
RATIO = (LENGTH_SCALE / SHORT_SCALE) ** 2
LOG_LONG = math.log2(AMPLITUDE)
LOG_SHORT = math.log2(SHORT_WEIGHT) - RATIO * LOG_LONG
PENALTY = -1024.0

NODES = np.cos((2.0 * np.arange(ORDER) + 1.0) * (math.pi / (2.0 * ORDER)))
NEIGHBOURS = [(i, j) for i in (-1, 0, 1) for j in (-1, 0, 1) if (i, j) != (0, 0)]


def lagrange_np(values):
    out = []
    for a in range(ORDER):
        col = np.ones_like(values)
        for b in range(ORDER):
            if b != a:
                col = col * (values - NODES[b]) / (NODES[a] - NODES[b])
        out.append(col)
    return np.stack(out, axis=-1)


def coupling_np(half, cell, reach):
    offsets = np.arange(-reach, reach + 1) * cell
    gap = half * NODES[None, :, None] - half * NODES[None, None, :] - offsets[:, None, None]
    total = 0.0
    for amp, scale in ((AMPLITUDE, LENGTH_SCALE), (SHORT_WEIGHT, SHORT_SCALE)):
        f = np.exp(-gap * gap / scale**2)
        total = total + amp * np.einsum("xad,ybe,zcf->xyzabcdef", f, f, f)
    n = 2 * reach + 1
    return total.reshape(n, n, n, RANK, RANK)


def leaf_weights():
    table = coupling_np(LEAF_HALF, 1.0, 3)
    w = np.zeros((49, B, RANK, B, RANK))
    for zs in range(B):
        for zt in range(B):
            w[:, zs, :, zt, :] = table[:, :, zs - zt + 3].reshape(49, RANK, RANK).transpose(0, 2, 1)
    return w.reshape(49 * B * RANK, B * RANK).astype(ml_dtypes.bfloat16)


def parent_weights():
    table = coupling_np(PARENT_HALF, 2.0, 2)
    w = np.zeros((26, 2, RANK, 2, RANK))
    for zs in range(2):
        for zt in range(2):
            w[:25, zs, :, zt, :] = table[:, :, zs - zt + 2].reshape(25, RANK, RANK).transpose(0, 2, 1)
    return w.reshape(26 * 2 * RANK, 2 * RANK).astype(ml_dtypes.bfloat16)


def transfer_weights():
    shifts = np.array([-0.5, 0.5])
    f = lagrange_np((shifts[:, None] + LEAF_HALF * NODES[None, :]) / PARENT_HALF)
    t = np.einsum("xad,ybe,zcf->xyzabcdef", f, f, f).reshape(2, 2, 2, RANK, RANK)
    up = np.zeros((2, 2, B, RANK, 2, RANK))
    for z in range(B):
        up[:, :, z, :, z // 2, :] = t[:, :, z % 2]
    up = up.reshape(4, B * RANK, 2 * RANK)
    return (
        up.reshape(4 * B * RANK, 2 * RANK).astype(ml_dtypes.bfloat16),
        up.transpose(2, 0, 1).reshape(2 * RANK, 4 * B * RANK).astype(ml_dtypes.bfloat16),
    )


def iota(shape, dim):
    return lax.broadcasted_iota(jnp.int32, shape, dim)


def dot_nt(a, b):
    return lax.dot_general(a, b, (((1,), (1,)), ((), ())), preferred_element_type=F32)


def split2(v):
    hi = v.astype(BF).astype(F32)
    return hi, (v - hi).astype(BF).astype(F32)


def prepare(gx, gy, coords_ref, charges_ref, order_ref, up_ref, cs_ref, np_ref, mb_ref, pm_ref, bb_ref):
    cen_x = (B * gx + 2).astype(F32)
    cen_y = (B * gy + 2).astype(F32)
    row8 = iota((8, WIDTH), 0)
    lane8 = iota((8, WIDTH), 1)
    lane_box = lane8 // PTS
    centre = jnp.where(row8 == 0, cen_x, jnp.where(row8 == 1, cen_y, 2.0))
    sources = []
    for c in range(16):
        q = charges_ref[:, c // B, c % B, :]
        xyz = coords_ref[:, c // B, c % B, :]
        xyz = jnp.concatenate([xyz, jnp.zeros((5, WIDTH), F32)], axis=0) - jnp.where(
            row8 < 3, centre, 0.0
        )
        sources.append((q, xyz))
    moments = []
    for c in range(16):
        x, y = c // B, c % B
        order = jnp.broadcast_to(order_ref[x, y : y + 1, :], (8, WIDTH))
        hi = order // WIDTH
        lo = order % WIDTH
        q = jnp.zeros((8, WIDTH), F32)
        xyz = jnp.zeros((8, WIDTH), F32)
        for k in range(16):
            here = hi == k
            q = jnp.where(here, jnp.take_along_axis(sources[k][0], lo, axis=1), q)
            xyz = jnp.where(here, jnp.take_along_axis(sources[k][1], lo, axis=1), xyz)
        cs_ref[c] = q
        q_low = q.astype(BF)
        hi2, lo2 = split2(xyz * SCALE)
        lo3 = jnp.concatenate([jnp.zeros((3, WIDTH), F32), lo2[0:5]], axis=0)
        feat = jnp.where(row8 < 3, hi2, lo3)
        np_ref[x, y] = jnp.concatenate([feat, q_low.astype(F32)], axis=0).astype(BF)

        box_centre = jnp.where(
            row8 == 0, x - 1.5, jnp.where(row8 == 1, y - 1.5, lane_box.astype(F32) - 1.5)
        )
        u = (xyz - box_centre) * (1.0 / LEAF_HALF)
        diffs = [u - float(NODES[k]) for k in range(ORDER)]
        polys = []
        for a in range(ORDER):
            denom = 1.0
            poly = None
            for b in range(ORDER):
                if b != a:
                    denom *= float(NODES[a] - NODES[b])
                    poly = diffs[b] if poly is None else poly * diffs[b]
            polys.append(poly * (1.0 / denom))

        def spread(k, d):
            return jnp.broadcast_to(polys[k][d : d + 1, :], (8, WIDTH))

        r4 = row8 % 4
        z8 = jnp.where(
            r4 < 2,
            jnp.where(r4 == 0, spread(0, 2), spread(1, 2)),
            jnp.where(r4 == 2, spread(2, 2), spread(3, 2)),
        )
        yz = [jnp.where(row8 < 4, spread(2 * j, 1), spread(2 * j + 1, 1)) * z8 for j in range(2)]
        basis = jnp.concatenate([spread(a, 0) * yz[j] for a in range(ORDER) for j in range(2)], axis=0)
        lane64 = iota((RANK, WIDTH), 1) // PTS
        wide = jnp.concatenate([jnp.where(lane64 == z, basis, 0.0) for z in range(B)], axis=0).astype(BF)
        bb_ref[c] = wide
        m = dot_nt(q_low, wide).astype(BF)
        moments.append(m)
        m32 = m.astype(F32)
        mb_ref[x, y] = jnp.concatenate([m32[:, :128], m32[:, 128:]], axis=0).astype(BF)
    for px in range(2):
        rows = []
        for py in range(2):
            kids = [moments[(2 * px + sx) * B + 2 * py + sy].astype(F32) for sx in range(2) for sy in range(2)]
            rows.append(jnp.concatenate(kids, axis=1))
        lhs = jnp.concatenate(rows, axis=0).astype(BF)
        pm_ref[px] = jnp.dot(lhs, up_ref[...], preferred_element_type=F32).astype(BF)


def cut(side, size, width):
    if side == 0:
        return pl.ds(0, size), pl.ds(width, size)
    if side > 0:
        return pl.ds(size - width, width), pl.ds(0, width)
    return pl.ds(0, width), pl.ds(width + size, width)


def decode(entries, log_y, first_x, first_y, reach, log_z):
    x = (entries >> (log_y + log_z)) - first_x + reach
    y = ((entries >> log_z) & ((1 << log_y) - 1)) - first_y + reach
    return x, y, entries & ((1 << log_z) - 1)


def one_bit(entries, position):
    return jnp.where(entries >= 0, jnp.int32(1) << jnp.clip(position, 0, 30), 0)


def main_kernel(
    count_g,
    count_d,
    log_y,
    coords_in,
    charges_in,
    order_in,
    near_in,
    far_in,
    coarse_in,
    up_in,
    wl_in,
    wp_in,
    down_in,
    out_ref,
    coords,
    charges,
    order,
    near_list,
    far_list,
    coarse_list,
    up,
    wl,
    wp,
    down,
    cs,
    np_in,
    mb_in,
    pm_in,
    basis,
    near_out,
    np_halo,
    mb_halo,
    pm_halo,
    win,
    lhs,
    words,
    targets,
    load_sem,
    send,
    recv,
):
    g = lax.axis_index("group")
    d = lax.axis_index("dev")

    def there(i, j):
        return (lax.rem(g + i + count_g, count_g), lax.rem(d + j + count_d, count_d))

    loads = [
        pltpu.make_async_copy(src, dst, load_sem.at[n])
        for n, (src, dst) in enumerate(
            (
                (coords_in, coords),
                (charges_in, charges),
                (order_in, order),
                (up_in, up),
                (near_in, near_list),
                (far_in, far_list),
                (coarse_in, coarse_list),
                (wp_in, wp),
                (down_in, down),
                (wl_in, wl),
            )
        )
    ]
    for load in loads:
        load.start()

    barrier = pltpu.get_barrier_semaphore()
    for i, j in NEIGHBOURS:
        pl.semaphore_signal(barrier, inc=1, device_id=there(i, j), device_id_type=MESH)
    for load in loads[:4]:
        load.wait()
    prepare(g, d, coords, charges, order, up, cs, np_in, mb_in, pm_in, basis)
    pl.semaphore_wait(barrier, len(NEIGHBOURS))

    def remote(n, k, src, dst):
        return pltpu.make_async_remote_copy(
            src_ref=src,
            dst_ref=dst,
            send_sem=send.at[n, k],
            recv_sem=recv.at[n, k],
            device_id=there(*NEIGHBOURS[n]),
            device_id_type=MESH,
        )

    near_copies, moment_copies, parent_copies = [], [], []
    for n, (i, j) in enumerate(NEIGHBOURS):
        (sx, tx), (sy, ty) = cut(i, B, 1), cut(j, B, 1)
        near_copies.append(remote(n, 0, np_in.at[sx, sy], np_halo.at[tx, ty]))
        (sx, tx), (sy, ty) = cut(i, B, 3), cut(j, B, 3)
        moment_copies.append(remote(n, 1, mb_in.at[sx, sy], mb_halo.at[tx, ty]))
        parent_copies.append(remote(n, 2, pm_in, pm_halo.at[pl.ds(2 * (1 - i), 2), 1 - j]))
    for copy in near_copies + moment_copies + parent_copies:
        copy.start()

    row8 = iota((8, WIDTH), 0)
    lane8 = iota((8, WIDTH), 1)
    lane_box = lane8 // PTS
    lane4 = iota((4, 128), 1)
    row16 = iota((16, 128), 0)
    zeros8 = jnp.zeros((8, WIDTH), F32)

    def column(tile, sx, sy):
        feat, charge = tile[0:8], tile[8:16]
        lo = jnp.concatenate([feat[3:6], jnp.zeros((5, WIDTH), F32)], axis=0)
        pos = jnp.where(row8 < 3, feat + lo, 0.0)
        if sx or sy:
            pos = pos + jnp.where(row8 == 0, B * SCALE * sx, jnp.where(row8 == 1, B * SCALE * sy, 0.0))
        hi, lo = split2(pos)
        tight = hi + lo
        norm = -0.5 * jnp.sum(tight * tight, axis=0, keepdims=True)
        return hi, lo, norm, charge.astype(BF)

    def three(v):
        h, m = split2(v)
        low = (v - h - m).astype(BF).astype(F32)
        return [jnp.broadcast_to(part, (8, WIDTH)) for part in (h, m, low)]

    def twice(v):
        return jnp.where(row8 < 3, v, jnp.concatenate([v[5:8], v[0:5]], axis=0))

    own_box = jnp.where(lane_box == row8 - 4, 1.0, 0.0)

    def source(col):
        hi, lo, norm, charge = col
        nh, nm, nl = three(norm)
        s0 = jnp.where(row8 < 6, twice(hi), jnp.where(row8 == 6, nh, nm))
        s1 = jnp.where(row8 < 6, twice(lo), jnp.where(row8 == 6, nl, 1.0))
        s2 = jnp.where(row8 < 2, 1.0, own_box)
        return jnp.concatenate([s0, s1, s2, zeros8], axis=0).astype(BF), charge

    def near_sums(sources, depth=1, width=4):
        groups = []
        for (x, y), features in sources.items():
            near = [
                (tx * B + ty, 3 * (x - tx) + y - ty)
                for tx in range(B)
                for ty in range(B)
                if 0 <= x - tx < 3 and 0 <= y - ty < 3
            ]
            groups += [(features, near[n : n + width]) for n in range(0, len(near), width)]
        acc = {}
        exponents, kernels = [], []

        def exponent(n):
            (feat, _), group = groups[n]
            return lax.dot_general(
                feat,
                jnp.concatenate([targets[c, slot] for c, slot in group], axis=1),
                (((0,), (0,)), ((), ())),
                preferred_element_type=F32,
            )

        def finish(n, kernel):
            (_, charge), group = groups[n]
            out = jnp.dot(charge, kernel, preferred_element_type=F32)
            for i, (c, _) in enumerate(group):
                part = out[:, 128 * i : 128 * i + 128]
                acc[c] = part if c not in acc else acc[c] + part

        waiting = []
        u = exponent(0)
        for n in range(len(groups)):
            after = exponent(n + 1) if n + 1 < len(groups) else None
            waiting.append((n, (jnp.exp2(u) + jnp.exp2(u * RATIO + LOG_SHORT)).astype(BF)))
            u = after
            if len(waiting) > depth:
                finish(*waiting.pop(0))
        for item in waiting:
            finish(*item)
        return acc

    def window(x, y, tile):
        for half in range(2):
            m = tile[8 * half : 8 * half + 8].astype(F32)
            turned = jnp.concatenate([m[4:8], m[0:4]], axis=0)
            first = jnp.where(row8 < 4, m, turned)
            last = jnp.where(row8 < 4, turned, m)
            lanes = slice(128 * half, 128 * half + 128)
            win[x, y, 0, :, lanes] = jnp.concatenate([first, first], axis=0).astype(BF)
            win[x, y, 1, :, lanes] = jnp.concatenate([last, last], axis=0).astype(BF)

    def lhs_at(x, dx, y, dy, s):
        row = x * 128 + y * 32 + 16 * s
        lane = dx * 1792 + 256 * dy
        return slice(row, row + 16), slice(lane, lane + 256)

    def is_own(x, dx, y, dy):
        return 3 <= x + dx < 7 and 3 <= y + dy < 7

    def products(keep, x, dx, y, dy):
        for s in range(2):
            lhs[lhs_at(x, dx, y, dy, s)] = keep * win[x + dx, y + dy, s]

    for load in loads[4:9]:
        load.wait()

    def far_words(x, carry):
        for y in range(B):
            entries = far_list[x, y]
            ox, oy, zs = decode(entries, log_y, B * g + x, B * d + y, 3, 2)
            slot = 7 * ox + oy
            late = slot >= 25
            bit = one_bit(entries, jnp.where(late, slot - 25, slot))
            for h in range(2):
                mine = jnp.where(late == (h == 1), bit, 0)
                w = [jnp.sum(jnp.where(zs == z, mine, 0), axis=1, keepdims=True) for z in range(B)]
                for half in range(2):
                    pair = jnp.where(
                        lane4 < 64,
                        jnp.broadcast_to(w[2 * half], (4, 128)),
                        jnp.broadcast_to(w[2 * half + 1], (4, 128)),
                    )
                    wide = jnp.broadcast_to(pair[0:1], (16, 128))
                    for z in range(1, B):
                        wide = jnp.where(row16 >= 4 * z, jnp.broadcast_to(pair[z : z + 1], (16, 128)), wide)
                    words[h, x, y, :, 128 * half : 128 * half + 128] = wide
        return carry

    lax.fori_loop(0, B, far_words, 0)

    def own_windows(x, carry):
        for y in range(B):
            window(x + 3, y + 3, mb_in[x, y])
        return carry

    lax.fori_loop(0, B, own_windows, 0)

    for x in range(B):
        for y in range(B):
            for h, first, last in ((0, 0, 25), (1, 25, 49)):
                w = words[h, x, y]
                for slot in range(first, last):
                    dx, dy = slot // 7, slot % 7
                    keep = jnp.where((w & (1 << (slot - first))) != 0, 1.0, 0.0).astype(BF)
                    if is_own(x, dx, y, dy):
                        products(keep, x, dx, y, dy)
                    else:
                        lhs[lhs_at(x, dx, y, dy, 0)] = keep

    own_source = {}
    for c in range(16):
        x, y = c // B, c % B
        col = column(np_in[x, y].astype(F32), 0, 0)
        own_source[x + 1, y + 1] = source(col)
        hi, lo, norm, _ = col
        nh, nm, nl = three(norm + LOG_LONG)
        a = jnp.where(row8 < 3, hi, jnp.concatenate([lo[5:8], lo[0:5]], axis=0))
        t0 = jnp.where(row8 < 6, a, 1.0)
        t1 = jnp.where(row8 < 6, a, jnp.where(row8 == 6, 1.0, nh))
        t2 = jnp.where(row8 == 0, nm, jnp.where(row8 == 1, nl, 0.0))

        entries = near_list[x, y]
        ox, oy, zs = decode(entries, log_y, B * g + x, B * d + y, 1, 2)
        bit = one_bit(entries, 3 * ox + oy + 9 * (zs & 1))
        lanes = []
        for h in range(2):
            w = jnp.sum(jnp.where((zs >> 1) == h, bit, 0), axis=1, keepdims=True)
            w = jnp.where(lane4 // PTS == iota((4, 128), 0), jnp.broadcast_to(w, (4, 128)), 0)
            lanes.append(jnp.broadcast_to(jnp.sum(w, axis=0, keepdims=True), (8, WIDTH)))
        word = jnp.where(row8 < 6, lanes[0], lanes[1])
        word = jnp.where(row8 % 2 == 1, word >> 9, word)
        for slot in range(9):
            pen = jnp.where((word & (1 << slot)) != 0, 0.0, PENALTY)
            t = [t0, t1, jnp.where(row8 < 4, t2, pen), zeros8]
            targets[c, slot] = jnp.concatenate(t, axis=0).astype(BF)
    for c, part in near_sums(own_source).items():
        near_out[c] = part

    pm_halo[pl.ds(2, 2), 1] = pm_in[...]

    for copy in near_copies:
        copy.wait_recv()
    halo_source = {}
    for x in range(6):
        for y in range(6):
            sx, sy = (x == 5) - (x == 0), (y == 5) - (y == 0)
            if sx or sy:
                halo_source[x, y] = source(column(np_halo[x, y].astype(F32), sx, sy))
    for c, part in near_sums(halo_source).items():
        near_out[c] = near_out[c] + part

    for copy in parent_copies:
        copy.wait_recv()
    lane2 = iota((2, 128), 1)
    rows = []
    for px in range(2):
        for py in range(2):
            entries = coarse_list[px, py]
            ox, oy, zs = decode(entries, log_y - 1, 2 * g + px, 2 * d + py, 2, 1)
            bit = one_bit(entries, 5 * ox + oy)
            w = [jnp.sum(jnp.where(zs == z, bit, 0), axis=1, keepdims=True) for z in range(2)]
            pair = jnp.where(lane2 < 64, jnp.broadcast_to(w[0], (2, 128)), jnp.broadcast_to(w[1], (2, 128)))
            wide = jnp.where(
                row16 < 8, jnp.broadcast_to(pair[0:1], (16, 128)), jnp.broadcast_to(pair[1:2], (16, 128))
            )
            parts = []
            for dx in range(5):
                for dy in range(5):
                    tile = pm_halo[px + dx, (py + dy) // 2].astype(F32)
                    r = 8 * ((py + dy) % 2)
                    m = tile[r : r + 8]
                    m = jnp.concatenate([m, m], axis=0)
                    parts.append(jnp.where((wide & (1 << (5 * dx + dy))) != 0, m, 0.0))
            parts.append(jnp.zeros((16, 128), F32))
            rows.append(jnp.concatenate(parts, axis=1).astype(BF))
    parent = jnp.dot(jnp.concatenate(rows, axis=0), wp[...], preferred_element_type=F32)
    picked = jnp.concatenate(
        [jnp.where(lane8 < 64, parent[16 * q : 16 * q + 8], parent[16 * q + 8 : 16 * q + 16]) for q in range(4)],
        axis=0,
    ).astype(BF)
    descent = jnp.dot(picked, down[...], preferred_element_type=F32)

    for copy in moment_copies:
        copy.wait_recv()
    loads[9].wait()

    def outer_windows(n, carry):
        x = n + 4 * (n // 3)
        for y in range(10):
            window(x, y, mb_halo[x, y])
        return carry

    lax.fori_loop(0, 6, outer_windows, 0)

    def side_windows(x, carry):
        for y in (0, 1, 2, 7, 8, 9):
            window(x, y, mb_halo[x, y])
        return carry

    lax.fori_loop(3, 7, side_windows, 0)

    for dx in range(7):
        for dy in range(7):
            for x in range(B):
                for y in range(B):
                    if not is_own(x, dx, y, dy):
                        products(lhs[lhs_at(x, dx, y, dy, 0)], x, dx, y, dy)
    local = jnp.dot(lhs[...], wl[...], preferred_element_type=F32)

    lane_z = iota((4, 256), 1) // RANK
    for c in range(16):
        x, y = c // B, c % B
        halves = []
        for s in range(2):
            block = local[c * 32 + 16 * s : c * 32 + 16 * s + 16]
            got = block[0:4]
            for z in range(1, B):
                got = jnp.where(lane_z == z, block[4 * z : 4 * z + 4], got)
            halves.append(got)
        q = (x // 2) * 2 + y // 2
        k = (x % 2) * 2 + y % 2
        total = jnp.concatenate(halves, axis=0) + descent[8 * q : 8 * q + 8, 256 * k : 256 * k + 256]
        far = jnp.dot(total.astype(BF), basis[c], preferred_element_type=F32)
        out_ref[:, x, y, :] = NUGGET * cs[c] + near_out[c] + far
    for copy in near_copies + moment_copies + parent_copies:
        copy.wait_send()


def vmem(n):
    return [pl.BlockSpec(memory_space=pltpu.VMEM)] * n


def anywhere(n):
    return [pl.BlockSpec(memory_space=pltpu.HBM)] * n


def params(mib, **kw):
    return pltpu.CompilerParams(vmem_limit_bytes=mib << 20, **kw)


def on_device(count_g, count_d, wl, wp, up, down, coords, charges, order, near_list, far_list, coarse_list):
    log_y = (count_d * B).bit_length() - 1
    near_list = near_list.transpose(1, 2, 3, 0)
    far_list = far_list.transpose(1, 2, 3, 0)
    coarse_list = coarse_list.transpose(1, 2, 3, 0)
    operands = (coords, charges, order, near_list, far_list, coarse_list, up, wl, wp, down)
    return pl.pallas_call(
        functools.partial(main_kernel, count_g, count_d, log_y),
        out_shape=pltpu.VMEM((RHS, B, B, WIDTH), F32),
        in_specs=[pl.BlockSpec(memory_space=pl.ANY)] * len(operands),
        out_specs=pl.BlockSpec(memory_space=pltpu.VMEM),
        scratch_shapes=[pltpu.VMEM(a.shape, a.dtype) for a in operands]
        + [
            pltpu.VMEM((16, RHS, WIDTH), F32),
            pltpu.VMEM((B, B, 16, WIDTH), BF),
            pltpu.VMEM((B, B, 16, 128), BF),
            pltpu.VMEM((2, 16, 128), BF),
            pltpu.VMEM((16, B * RANK, WIDTH), BF),
            pltpu.VMEM((16, RHS, WIDTH), F32),
            pltpu.VMEM((6, 6, 16, WIDTH), BF),
            pltpu.VMEM((10, 10, 16, 128), BF),
            pltpu.VMEM((6, 3, 16, 128), BF),
            pltpu.VMEM((10, 10, 2, 16, 256), BF),
            pltpu.VMEM((512, 49 * 256), BF),
            pltpu.VMEM((2, B, B, 16, 256), jnp.int32),
            pltpu.VMEM((16, 9, 32, WIDTH), BF),
            pltpu.SemaphoreType.DMA((len(operands),)),
            pltpu.SemaphoreType.DMA((8, 3)),
            pltpu.SemaphoreType.DMA((8, 3)),
        ],
        compiler_params=pltpu.CompilerParams(
            vmem_limit_bytes=60 << 20, collective_id=0, has_side_effects=True
        ),
        name="fields",
    )(*operands)


def solution(mesh):
    placed = (
        P(None, "group", "dev", None),
        P(None, "group", "dev", None),
        P("group", "dev", None),
        P(None, "group", "dev", None),
        P(None, "group", "dev", None),
        P(None, "group", "dev", None),
    )
    up, down = transfer_weights()
    wl, wp = leaf_weights(), parent_weights()

    def body(*args):
        return on_device(
            mesh.shape["group"],
            mesh.shape["dev"],
            jnp.asarray(wl),
            jnp.asarray(wp),
            jnp.asarray(up),
            jnp.asarray(down),
            *args,
        )

    return jax.shard_map(
        body,
        mesh=mesh,
        in_specs=placed,
        out_specs=P(None, "group", "dev", None),
        check_vma=False,
    )
```

```python
import functools
import math

import jax
import jax.numpy as jnp
import ml_dtypes
import numpy as np
from jax import lax
from jax.experimental import pallas as pl
from jax.experimental.pallas import tpu as pltpu
from jax.sharding import PartitionSpec as P

MESH = pl.DeviceIdType.MESH
BF = jnp.bfloat16
F32 = jnp.float32

ORDER = 4
LENGTH_SCALE = 2.5
AMPLITUDE = 0.025
SHORT_SCALE = 0.5
SHORT_WEIGHT = 0.1
NUGGET = 0.5
LEAF_HALF = 0.75
PARENT_HALF = 1.25

B = 4
PTS = 32
WIDTH = B * PTS
RHS = 8
RANK = ORDER**3

KAPPA = math.log2(math.e) / LENGTH_SCALE**2
SCALE = math.sqrt(2.0 * KAPPA)
RATIO = (LENGTH_SCALE / SHORT_SCALE) ** 2
LOG_LONG = math.log2(AMPLITUDE)
LOG_SHORT = math.log2(SHORT_WEIGHT) - RATIO * LOG_LONG
PENALTY = -1024.0

NODES = np.cos((2.0 * np.arange(ORDER) + 1.0) * (math.pi / (2.0 * ORDER)))
NEIGHBOURS = [(i, j) for i in (-1, 0, 1) for j in (-1, 0, 1) if (i, j) != (0, 0)]


def lagrange_np(values):
    out = []
    for a in range(ORDER):
        col = np.ones_like(values)
        for b in range(ORDER):
            if b != a:
                col = col * (values - NODES[b]) / (NODES[a] - NODES[b])
        out.append(col)
    return np.stack(out, axis=-1)


def coupling_np(half, cell, reach):
    offsets = np.arange(-reach, reach + 1) * cell
    gap = half * NODES[None, :, None] - half * NODES[None, None, :] - offsets[:, None, None]
    total = 0.0
    for amp, scale in ((AMPLITUDE, LENGTH_SCALE), (SHORT_WEIGHT, SHORT_SCALE)):
        f = np.exp(-gap * gap / scale**2)
        total = total + amp * np.einsum("xad,ybe,zcf->xyzabcdef", f, f, f)
    n = 2 * reach + 1
    return total.reshape(n, n, n, RANK, RANK)


def leaf_weights():
    table = coupling_np(LEAF_HALF, 1.0, 3)
    w = np.zeros((49, B, RANK, B, RANK))
    for zs in range(B):
        for zt in range(B):
            w[:, zs, :, zt, :] = table[:, :, zs - zt + 3].reshape(49, RANK, RANK).transpose(0, 2, 1)
    return w.reshape(49 * B * RANK, B * RANK).astype(ml_dtypes.bfloat16)


def parent_weights():
    table = coupling_np(PARENT_HALF, 2.0, 2)
    w = np.zeros((26, 2, RANK, 2, RANK))
    for zs in range(2):
        for zt in range(2):
            w[:25, zs, :, zt, :] = table[:, :, zs - zt + 2].reshape(25, RANK, RANK).transpose(0, 2, 1)
    return w.reshape(26 * 2 * RANK, 2 * RANK).astype(ml_dtypes.bfloat16)


def transfer_weights():
    shifts = np.array([-0.5, 0.5])
    f = lagrange_np((shifts[:, None] + LEAF_HALF * NODES[None, :]) / PARENT_HALF)
    t = np.einsum("xad,ybe,zcf->xyzabcdef", f, f, f).reshape(2, 2, 2, RANK, RANK)
    up = np.zeros((2, 2, B, RANK, 2, RANK))
    for z in range(B):
        up[:, :, z, :, z // 2, :] = t[:, :, z % 2]
    up = up.reshape(4, B * RANK, 2 * RANK)
    return (
        up.reshape(4 * B * RANK, 2 * RANK).astype(ml_dtypes.bfloat16),
        up.transpose(2, 0, 1).reshape(2 * RANK, 4 * B * RANK).astype(ml_dtypes.bfloat16),
    )


def iota(shape, dim):
    return lax.broadcasted_iota(jnp.int32, shape, dim)


def dot_nt(a, b):
    return lax.dot_general(a, b, (((1,), (1,)), ((), ())), preferred_element_type=F32)


def split2(v):
    hi = v.astype(BF).astype(F32)
    return hi, (v - hi).astype(BF).astype(F32)


def prepare(gx, gy, coords_ref, charges_ref, order_ref, up_ref, cs_ref, np_ref, mb_ref, pm_ref, bb_ref):
    cen_x = (B * gx + 2).astype(F32)
    cen_y = (B * gy + 2).astype(F32)
    row8 = iota((8, WIDTH), 0)
    lane8 = iota((8, WIDTH), 1)
    lane_box = lane8 // PTS
    centre = jnp.where(row8 == 0, cen_x, jnp.where(row8 == 1, cen_y, 2.0))
    sources = []
    for c in range(16):
        q = charges_ref[:, c // B, c % B, :]
        xyz = coords_ref[:, c // B, c % B, :]
        xyz = jnp.concatenate([xyz, jnp.zeros((5, WIDTH), F32)], axis=0) - jnp.where(
            row8 < 3, centre, 0.0
        )
        sources.append((q, xyz))
    moments = []
    for c in range(16):
        x, y = c // B, c % B
        order = jnp.broadcast_to(order_ref[x, y : y + 1, :], (8, WIDTH))
        hi = order // WIDTH
        lo = order % WIDTH
        q = jnp.zeros((8, WIDTH), F32)
        xyz = jnp.zeros((8, WIDTH), F32)
        for k in range(16):
            here = hi == k
            q = jnp.where(here, jnp.take_along_axis(sources[k][0], lo, axis=1), q)
            xyz = jnp.where(here, jnp.take_along_axis(sources[k][1], lo, axis=1), xyz)
        cs_ref[c] = q
        q_low = q.astype(BF)
        hi2, lo2 = split2(xyz * SCALE)
        lo3 = jnp.concatenate([jnp.zeros((3, WIDTH), F32), lo2[0:5]], axis=0)
        feat = jnp.where(row8 < 3, hi2, lo3)
        np_ref[x, y] = jnp.concatenate([feat, q_low.astype(F32)], axis=0).astype(BF)

        box_centre = jnp.where(
            row8 == 0, x - 1.5, jnp.where(row8 == 1, y - 1.5, lane_box.astype(F32) - 1.5)
        )
        u = (xyz - box_centre) * (1.0 / LEAF_HALF)
        diffs = [u - float(NODES[k]) for k in range(ORDER)]
        polys = []
        for a in range(ORDER):
            denom = 1.0
            poly = None
            for b in range(ORDER):
                if b != a:
                    denom *= float(NODES[a] - NODES[b])
                    poly = diffs[b] if poly is None else poly * diffs[b]
            polys.append(poly * (1.0 / denom))

        def spread(k, d):
            return jnp.broadcast_to(polys[k][d : d + 1, :], (8, WIDTH))

        r4 = row8 % 4
        z8 = jnp.where(
            r4 < 2,
            jnp.where(r4 == 0, spread(0, 2), spread(1, 2)),
            jnp.where(r4 == 2, spread(2, 2), spread(3, 2)),
        )
        yz = [jnp.where(row8 < 4, spread(2 * j, 1), spread(2 * j + 1, 1)) * z8 for j in range(2)]
        basis = jnp.concatenate([spread(a, 0) * yz[j] for a in range(ORDER) for j in range(2)], axis=0)
        lane64 = iota((RANK, WIDTH), 1) // PTS
        wide = jnp.concatenate([jnp.where(lane64 == z, basis, 0.0) for z in range(B)], axis=0).astype(BF)
        bb_ref[c] = wide
        m = dot_nt(q_low, wide).astype(BF)
        moments.append(m)
        m32 = m.astype(F32)
        mb_ref[x, y] = jnp.concatenate([m32[:, :128], m32[:, 128:]], axis=0).astype(BF)
    for px in range(2):
        rows = []
        for py in range(2):
            kids = [moments[(2 * px + sx) * B + 2 * py + sy].astype(F32) for sx in range(2) for sy in range(2)]
            rows.append(jnp.concatenate(kids, axis=1))
        lhs = jnp.concatenate(rows, axis=0).astype(BF)
        pm_ref[px] = jnp.dot(lhs, up_ref[...], preferred_element_type=F32).astype(BF)


def cut(side, size, width):
    if side == 0:
        return pl.ds(0, size), pl.ds(width, size)
    if side > 0:
        return pl.ds(size - width, width), pl.ds(0, width)
    return pl.ds(0, width), pl.ds(width + size, width)


def decode(entries, log_y, first_x, first_y, reach, log_z):
    x = (entries >> (log_y + log_z)) - first_x + reach
    y = ((entries >> log_z) & ((1 << log_y) - 1)) - first_y + reach
    return x, y, entries & ((1 << log_z) - 1)


def one_bit(entries, position):
    return jnp.where(entries >= 0, jnp.int32(1) << jnp.clip(position, 0, 30), 0)


def main_kernel(
    count_g,
    count_d,
    log_y,
    coords_in,
    charges_in,
    order_in,
    near_in,
    far_in,
    coarse_in,
    up_in,
    wl_in,
    wp_in,
    down_in,
    out_ref,
    coords,
    charges,
    order,
    near_list,
    far_list,
    coarse_list,
    up,
    wl,
    wp,
    down,
    cs,
    np_in,
    mb_in,
    pm_in,
    basis,
    near_out,
    np_halo,
    mb_halo,
    pm_halo,
    win,
    lhs,
    words,
    targets,
    load_sem,
    send,
    recv,
):
    g = lax.axis_index("group")
    d = lax.axis_index("dev")

    def there(i, j):
        return (lax.rem(g + i + count_g, count_g), lax.rem(d + j + count_d, count_d))

    loads = [
        pltpu.make_async_copy(src, dst, load_sem.at[n])
        for n, (src, dst) in enumerate(
            (
                (coords_in, coords),
                (charges_in, charges),
                (order_in, order),
                (up_in, up),
                (near_in, near_list),
                (far_in, far_list),
                (coarse_in, coarse_list),
                (wp_in, wp),
                (down_in, down),
                (wl_in, wl),
            )
        )
    ]
    for load in loads:
        load.start()

    barrier = pltpu.get_barrier_semaphore()
    for i, j in NEIGHBOURS:
        pl.semaphore_signal(barrier, inc=1, device_id=there(i, j), device_id_type=MESH)
    for load in loads[:4]:
        load.wait()
    prepare(g, d, coords, charges, order, up, cs, np_in, mb_in, pm_in, basis)
    pl.semaphore_wait(barrier, len(NEIGHBOURS))

    def remote(n, k, src, dst):
        return pltpu.make_async_remote_copy(
            src_ref=src,
            dst_ref=dst,
            send_sem=send.at[n, k],
            recv_sem=recv.at[n, k],
            device_id=there(*NEIGHBOURS[n]),
            device_id_type=MESH,
        )

    near_copies, moment_copies, parent_copies = [], [], []
    for n, (i, j) in enumerate(NEIGHBOURS):
        (sx, tx), (sy, ty) = cut(i, B, 1), cut(j, B, 1)
        near_copies.append(remote(n, 0, np_in.at[sx, sy], np_halo.at[tx, ty]))
        (sx, tx), (sy, ty) = cut(i, B, 3), cut(j, B, 3)
        moment_copies.append(remote(n, 1, mb_in.at[sx, sy], mb_halo.at[tx, ty]))
        parent_copies.append(remote(n, 2, pm_in, pm_halo.at[pl.ds(2 * (1 - i), 2), 1 - j]))
    for copy in near_copies + moment_copies + parent_copies:
        copy.start()

    row8 = iota((8, WIDTH), 0)
    lane8 = iota((8, WIDTH), 1)
    lane_box = lane8 // PTS
    lane4 = iota((4, 128), 1)
    row16 = iota((16, 128), 0)
    zeros8 = jnp.zeros((8, WIDTH), F32)

    def column(tile, sx, sy):
        feat, charge = tile[0:8], tile[8:16]
        lo = jnp.concatenate([feat[3:6], jnp.zeros((5, WIDTH), F32)], axis=0)
        pos = jnp.where(row8 < 3, feat + lo, 0.0)
        if sx or sy:
            pos = pos + jnp.where(row8 == 0, B * SCALE * sx, jnp.where(row8 == 1, B * SCALE * sy, 0.0))
        hi, lo = split2(pos)
        tight = hi + lo
        norm = -0.5 * jnp.sum(tight * tight, axis=0, keepdims=True)
        return hi, lo, norm, charge.astype(BF)

    def three(v):
        h, m = split2(v)
        low = (v - h - m).astype(BF).astype(F32)
        return [jnp.broadcast_to(part, (8, WIDTH)) for part in (h, m, low)]

    def twice(v):
        return jnp.where(row8 < 3, v, jnp.concatenate([v[5:8], v[0:5]], axis=0))

    own_box = jnp.where(lane_box == row8 - 4, 1.0, 0.0)

    def source(col):
        hi, lo, norm, charge = col
        nh, nm, nl = three(norm)
        s0 = jnp.where(row8 < 6, twice(hi), jnp.where(row8 == 6, nh, nm))
        s1 = jnp.where(row8 < 6, twice(lo), jnp.where(row8 == 6, nl, 1.0))
        s2 = jnp.where(row8 < 2, 1.0, own_box)
        return jnp.concatenate([s0, s1, s2, zeros8], axis=0).astype(BF), charge

    def near_sums(sources, depth=2, width=4):
        groups = []
        for (x, y), features in sources.items():
            near = [
                (tx * B + ty, 3 * (x - tx) + y - ty)
                for tx in range(B)
                for ty in range(B)
                if 0 <= x - tx < 3 and 0 <= y - ty < 3
            ]
            groups += [(features, near[n : n + width]) for n in range(0, len(near), width)]
        acc = {}
        exponents, kernels = [], []

        def exponent(n):
            (feat, _), group = groups[n]
            return lax.dot_general(
                feat,
                jnp.concatenate([targets[c, slot] for c, slot in group], axis=1),
                (((0,), (0,)), ((), ())),
                preferred_element_type=F32,
            )

        def finish(n, kernel):
            (_, charge), group = groups[n]
            out = jnp.dot(charge, kernel, preferred_element_type=F32)
            for i, (c, _) in enumerate(group):
                part = out[:, 128 * i : 128 * i + 128]
                acc[c] = part if c not in acc else acc[c] + part

        waiting = []
        u = exponent(0)
        for n in range(len(groups)):
            after = exponent(n + 1) if n + 1 < len(groups) else None
            waiting.append((n, (jnp.exp2(u) + jnp.exp2(u * RATIO + LOG_SHORT)).astype(BF)))
            u = after
            if len(waiting) > depth:
                finish(*waiting.pop(0))
        for item in waiting:
            finish(*item)
        return acc

    def window(x, y, tile):
        for half in range(2):
            m = tile[8 * half : 8 * half + 8].astype(F32)
            win[x, y, :, 128 * half : 128 * half + 128] = jnp.concatenate([m, m], axis=0).astype(BF)

    def is_own(x, dx, y, dy):
        return 3 <= x + dx < 7 and 3 <= y + dy < 7

    none = jnp.zeros((16, 256), BF)

    def products(x, dx, y, dy):
        slot = 7 * dx + dy
        for zp in range(2):
            row, lane = 256 * zp + 16 * (x * B + y), 256 * slot
            keep = (words[slot // 13, x, y, zp] & jnp.int16(1 << (slot % 13))) != jnp.int16(0)
            lhs[row : row + 16, lane : lane + 256] = jnp.where(keep, win[x + dx, y + dy], none)

    for load in loads[4:9]:
        load.wait()

    def far_words(x, carry):
        for y in range(B):
            entries = far_list[x, y]
            ox, oy, zs = decode(entries, log_y, B * g + x, B * d + y, 3, 2)
            slot = 7 * ox + oy
            part = jnp.where(slot >= 26, jnp.where(slot >= 39, 3, 2), jnp.where(slot >= 13, 1, 0))
            bit = one_bit(entries, slot - 13 * part)
            for h in range(4):
                mine = jnp.where(part == h, bit, 0)
                w = [jnp.sum(jnp.where(zs == z, mine, 0), axis=1, keepdims=True) for z in range(B)]
                for half in range(2):
                    pair = jnp.where(
                        lane4 < 64,
                        jnp.broadcast_to(w[2 * half], (4, 128)),
                        jnp.broadcast_to(w[2 * half + 1], (4, 128)),
                    )
                    for zp in range(2):
                        wide = jnp.where(
                            row16 < 8,
                            jnp.broadcast_to(pair[2 * zp : 2 * zp + 1], (16, 128)),
                            jnp.broadcast_to(pair[2 * zp + 1 : 2 * zp + 2], (16, 128)),
                        )
                        words[h, x, y, zp, :, 128 * half : 128 * half + 128] = wide.astype(jnp.int16)
        return carry

    lax.fori_loop(0, B, far_words, 0)

    def own_windows(x, carry):
        for y in range(B):
            window(x + 3, y + 3, mb_in[x, y])
        return carry

    lax.fori_loop(0, B, own_windows, 0)

    for x in range(B):
        for y in range(B):
            for dx in range(3 - x, 7 - x):
                for dy in range(3 - y, 7 - y):
                    products(x, dx, y, dy)

    own_source = {}
    for c in range(16):
        x, y = c // B, c % B
        col = column(np_in[x, y].astype(F32), 0, 0)
        own_source[x + 1, y + 1] = source(col)
        hi, lo, norm, _ = col
        nh, nm, nl = three(norm + LOG_LONG)
        a = jnp.where(row8 < 3, hi, jnp.concatenate([lo[5:8], lo[0:5]], axis=0))
        t0 = jnp.where(row8 < 6, a, 1.0)
        t1 = jnp.where(row8 < 6, a, jnp.where(row8 == 6, 1.0, nh))
        t2 = jnp.where(row8 == 0, nm, jnp.where(row8 == 1, nl, 0.0))

        entries = near_list[x, y]
        ox, oy, zs = decode(entries, log_y, B * g + x, B * d + y, 1, 2)
        bit = one_bit(entries, 3 * ox + oy + 9 * (zs & 1))
        lanes = []
        for h in range(2):
            w = jnp.sum(jnp.where((zs >> 1) == h, bit, 0), axis=1, keepdims=True)
            w = jnp.where(lane4 // PTS == iota((4, 128), 0), jnp.broadcast_to(w, (4, 128)), 0)
            lanes.append(jnp.broadcast_to(jnp.sum(w, axis=0, keepdims=True), (8, WIDTH)))
        word = jnp.where(row8 < 6, lanes[0], lanes[1])
        word = jnp.where(row8 % 2 == 1, word >> 9, word)
        for slot in range(9):
            pen = jnp.where((word & (1 << slot)) != 0, 0.0, PENALTY)
            t = [t0, t1, jnp.where(row8 < 4, t2, pen), zeros8]
            targets[c, slot] = jnp.concatenate(t, axis=0).astype(BF)
    for c, part in near_sums(own_source).items():
        near_out[c] = part

    pm_halo[pl.ds(2, 2), 1] = pm_in[...]

    for copy in near_copies:
        copy.wait_recv()
    halo_source = {}
    for x in range(6):
        for y in range(6):
            sx, sy = (x == 5) - (x == 0), (y == 5) - (y == 0)
            if sx or sy:
                halo_source[x, y] = source(column(np_halo[x, y].astype(F32), sx, sy))
    for c, part in near_sums(halo_source).items():
        near_out[c] = near_out[c] + part

    for copy in parent_copies:
        copy.wait_recv()
    lane2 = iota((2, 128), 1)
    rows = []
    for px in range(2):
        for py in range(2):
            entries = coarse_list[px, py]
            ox, oy, zs = decode(entries, log_y - 1, 2 * g + px, 2 * d + py, 2, 1)
            bit = one_bit(entries, 5 * ox + oy)
            w = [jnp.sum(jnp.where(zs == z, bit, 0), axis=1, keepdims=True) for z in range(2)]
            pair = jnp.where(lane2 < 64, jnp.broadcast_to(w[0], (2, 128)), jnp.broadcast_to(w[1], (2, 128)))
            wide = jnp.where(
                row16 < 8, jnp.broadcast_to(pair[0:1], (16, 128)), jnp.broadcast_to(pair[1:2], (16, 128))
            )
            parts = []
            for dx in range(5):
                for dy in range(5):
                    tile = pm_halo[px + dx, (py + dy) // 2].astype(F32)
                    r = 8 * ((py + dy) % 2)
                    m = tile[r : r + 8]
                    m = jnp.concatenate([m, m], axis=0)
                    parts.append(jnp.where((wide & (1 << (5 * dx + dy))) != 0, m, 0.0))
            parts.append(jnp.zeros((16, 128), F32))
            rows.append(jnp.concatenate(parts, axis=1).astype(BF))
    parent = jnp.dot(jnp.concatenate(rows, axis=0), wp[...], preferred_element_type=F32)
    picked = jnp.concatenate(
        [jnp.where(lane8 < 64, parent[16 * q : 16 * q + 8], parent[16 * q + 8 : 16 * q + 16]) for q in range(4)],
        axis=0,
    ).astype(BF)
    descent = jnp.dot(picked, down[...], preferred_element_type=F32)

    for copy in moment_copies:
        copy.wait_recv()
    loads[9].wait()

    def outer_windows(n, carry):
        x = n + 4 * (n // 3)
        for y in range(10):
            window(x, y, mb_halo[x, y])
        return carry

    lax.fori_loop(0, 6, outer_windows, 0)

    def side_windows(x, carry):
        for y in (0, 1, 2, 7, 8, 9):
            window(x, y, mb_halo[x, y])
        return carry

    lax.fori_loop(3, 7, side_windows, 0)

    for dx in range(7):
        for dy in range(7):
            for x in range(B):
                for y in range(B):
                    if not is_own(x, dx, y, dy):
                        products(x, dx, y, dy)
    local = [
        jnp.dot(
            lhs[256 * zp : 256 * zp + 256, :], wl[:, 128 * zp : 128 * zp + 128], preferred_element_type=F32
        )
        for zp in range(2)
    ]

    for c in range(16):
        x, y = c // B, c % B
        halves = [jnp.where(lane8 < 64, v[16 * c : 16 * c + 8], v[16 * c + 8 : 16 * c + 16]) for v in local]
        q = (x // 2) * 2 + y // 2
        k = (x % 2) * 2 + y % 2
        total = jnp.concatenate(halves, axis=1) + descent[8 * q : 8 * q + 8, 256 * k : 256 * k + 256]
        far = jnp.dot(total.astype(BF), basis[c], preferred_element_type=F32)
        out_ref[:, x, y, :] = NUGGET * cs[c] + near_out[c] + far
    for copy in near_copies + moment_copies + parent_copies:
        copy.wait_send()


def vmem(n):
    return [pl.BlockSpec(memory_space=pltpu.VMEM)] * n


def anywhere(n):
    return [pl.BlockSpec(memory_space=pltpu.HBM)] * n


def params(mib, **kw):
    return pltpu.CompilerParams(vmem_limit_bytes=mib << 20, **kw)


def on_device(count_g, count_d, wl, wp, up, down, coords, charges, order, near_list, far_list, coarse_list):
    log_y = (count_d * B).bit_length() - 1
    near_list = near_list.transpose(1, 2, 3, 0)
    far_list = far_list.transpose(1, 2, 3, 0)
    coarse_list = coarse_list.transpose(1, 2, 3, 0)
    operands = (coords, charges, order, near_list, far_list, coarse_list, up, wl, wp, down)
    return pl.pallas_call(
        functools.partial(main_kernel, count_g, count_d, log_y),
        out_shape=pltpu.VMEM((RHS, B, B, WIDTH), F32),
        in_specs=[pl.BlockSpec(memory_space=pl.ANY)] * len(operands),
        out_specs=pl.BlockSpec(memory_space=pltpu.VMEM),
        scratch_shapes=[pltpu.VMEM(a.shape, a.dtype) for a in operands]
        + [
            pltpu.VMEM((16, RHS, WIDTH), F32),
            pltpu.VMEM((B, B, 16, WIDTH), BF),
            pltpu.VMEM((B, B, 16, 128), BF),
            pltpu.VMEM((2, 16, 128), BF),
            pltpu.VMEM((16, B * RANK, WIDTH), BF),
            pltpu.VMEM((16, RHS, WIDTH), F32),
            pltpu.VMEM((6, 6, 16, WIDTH), BF),
            pltpu.VMEM((10, 10, 16, 128), BF),
            pltpu.VMEM((6, 3, 16, 128), BF),
            pltpu.VMEM((10, 10, 16, 256), BF),
            pltpu.VMEM((512, 49 * 256), BF),
            pltpu.VMEM((4, B, B, 2, 16, 256), jnp.int16),
            pltpu.VMEM((16, 9, 32, WIDTH), BF),
            pltpu.SemaphoreType.DMA((len(operands),)),
            pltpu.SemaphoreType.DMA((8, 3)),
            pltpu.SemaphoreType.DMA((8, 3)),
        ],
        compiler_params=pltpu.CompilerParams(
            vmem_limit_bytes=60 << 20, collective_id=0, has_side_effects=True
        ),
        name="fields",
    )(*operands)


def solution(mesh):
    placed = (
        P(None, "group", "dev", None),
        P(None, "group", "dev", None),
        P("group", "dev", None),
        P(None, "group", "dev", None),
        P(None, "group", "dev", None),
        P(None, "group", "dev", None),
    )
    up, down = transfer_weights()
    wl, wp = leaf_weights(), parent_weights()

    def body(*args):
        return on_device(
            mesh.shape["group"],
            mesh.shape["dev"],
            jnp.asarray(wl),
            jnp.asarray(wp),
            jnp.asarray(up),
            jnp.asarray(down),
            *args,
        )

    return jax.shard_map(
        body,
        mesh=mesh,
        in_specs=placed,
        out_specs=P(None, "group", "dev", None),
        check_vma=False,
    )
```
